128 devices in a mesh: box: 8 (over z_hi, x), samp: 16 (over y, z_lo, core).
Axes of the slice: x: 4, y: 4, z: 4 (z_hi: 2, z_lo: 2; z = z_hi * 2 + z_lo), core: 2. Of those that a mesh axis runs over, the one named last changes fastest.
Arguments:
- child_patterns: float32 [1024, 2, 128, 256], P(('box', 'samp')), may hold values from -6 to 6
- octants: int32 [1024], P(('box', 'samp')), may hold values from 0 to 7
- parent_map: int32 [8, 128], P('box'), may hold values from 0 to 31, never falling along the last dimension, each value on 1 to 8 neighbouring positions
- far_boxes: int32 [256, 48], P('box'), may hold values from 0 to 255, as said below
- offsets: int32 [256, 48], P('box'), may hold values from 0 to 315
- translation: float32 [316, 2, 192, 384], P(None, None, 'samp'), may hold values from -0.5 to 0.5
Outputs:
- outgoing: float32 [256, 2, 192, 384], P('box', None, 'samp')
- incoming: float32 [256, 2, 192, 384], P('box', None, 'samp')
The draws below stay inside these ranges and needn't reach their ends.
Inputs may be any that keep to these rules, and one draw needn't show every extreme that they name: `parent_map`: each row never falls, and every parent of a box group has 1 to 8 children. `far_boxes`: row p lists 48 different parent boxes, none equal to p.
All inputs are finite; a program needn't handle non-finite values.
Results may differ from the reference program's by a relative error of at most 0.0003.
Values sent between devices are 32-bit elements; how exact they have to be, the bound alone decides.
No kernel may reach another device: no remote copies, remote signals or barrier semaphores. Data moves between devices by JAX's collectives and lax.ppermute only.
A program may use at most 128 MiB of HBM per device.

```python
import math
import jax
import jax.numpy as jnp
import numpy as np
from jax import lax

NT1 = 128
NP1 = 256
NT2 = 192
NP2 = 384
NOFF = 316
NI = 48
CHILD_GRP = 128
PAR_GRP = 32
CHILDREN = 1024
PARENTS = 256
N_BOX = 8


def draw_far_boxes(key, part):
    key = jax.random.fold_in(key, 11)
    row_keys = jax.random.split(key, PARENTS)

    def one_row(row_key):
        shuffled = jax.random.permutation(row_key, PARENTS - 2) + 1
        return jnp.concatenate([jnp.zeros((1,), jnp.int32), shuffled[:NI - 1].astype(jnp.int32)])
    steps_ahead = jax.vmap(one_row)(row_keys)
    owners = jnp.arange(PARENTS, dtype=jnp.int32)[:, None]
    return ((owners + 1 + steps_ahead) % PARENTS).astype(jnp.int32)


def with_ends(array, stream_key, low, top_value):
    longest = array.shape.index(max(array.shape))
    spots = []
    for shift in (0, 1):
        where = [jax.random.randint(jax.random.fold_in(stream_key, axis), (), 0, length) for axis, length in enumerate(array.shape)]
        where[longest] = (where[longest] + shift) % array.shape[longest]
        spots.append(tuple(where))
    return array.at[spots[0]].set(low).at[spots[1]].set(top_value)


def steps_of(own_key, dims, cuts, least, top_value):
    loudness = 1.0
    for dim, parts in cuts:
        draws = jax.random.uniform(jax.random.fold_in(jax.random.fold_in(own_key, 6), dim), (parts,), jnp.float32, least / len(cuts), top_value / len(cuts))
        loudness = loudness * jnp.repeat(jnp.exp(draws), dims[dim] // parts).reshape((-1,) + (1,) * (len(dims) - 1 - dim))
    return loudness


def profile(number_of, total, bound, lean):
    weights = [(1 << 20) // math.isqrt(grade ** lean) + 1 for grade in range(2, number_of + 1)]
    surplus, given = total - bound - (number_of - 1), [1] * (number_of - 1)
    while surplus > 0:
        candidates = [i for i in range(number_of - 1) if given[i] < bound]
        whole, left = sum([weights[i] for i in candidates]), surplus
        for i in candidates:
            more = min(bound - given[i], max(1, left * weights[i] // whole), surplus)
            given[i] = given[i] + more
            surplus = surplus - more
    return np.array([bound] + given)


def uneven_parts(own_key, number_of, total, bound, skew):
    if number_of == 2:
        one = jax.random.randint(own_key, (), max(1, total - bound), min(bound, total - 1) + 1)
        return jnp.stack([one, total - one])
    lengths = jnp.asarray(profile(number_of, total, bound, skew), jnp.int32)
    pairs = (number_of - 1) // 2
    donor, sink = lengths[1:1 + 2 * pairs:2], lengths[2:2 + 2 * pairs:2]
    room = jnp.minimum(donor - 1, bound - sink)
    passed = jax.random.randint(jax.random.fold_in(own_key, 1), (pairs,), 0, 1 << 20) % (room + 1)
    lengths = lengths.at[1:1 + 2 * pairs:2].set(donor - passed).at[2:2 + 2 * pairs:2].set(sink + passed)
    return lengths[jax.random.permutation(jax.random.fold_in(own_key, 2), number_of)]


def normal_values(key, extent, width, most, cuts=(), kind=jnp.bfloat16):
    result = jax.random.normal(key, extent, jnp.float32) * width
    if len(cuts) > 0:
        result = steps_of(key, extent, cuts, -0.22, 0.18) * result
    return jnp.clip(result, min=-most, max=most).astype(kind)


def setup_inputs(seed: int = 0) -> dict:
    streams_of = jax.random.split(jax.random.key(seed), 7)
    child_patterns = normal_values(streams_of[0], (CHILDREN, 2, NT1, NP1), 1.0, 6.0, ((0, 128),), jnp.float32)
    octants = with_ends(jax.random.randint(streams_of[1], (CHILDREN,), 0, 8), jax.random.fold_in(streams_of[1], 1), 0, 7).astype(jnp.int32)
    parent_map = jax.vmap(lambda own: jnp.searchsorted(jnp.cumsum(uneven_parts(own, PAR_GRP, CHILD_GRP, 8, 0)), jnp.arange(CHILD_GRP), side="right"))(jax.random.split(streams_of[2], N_BOX)).reshape((N_BOX, CHILD_GRP)).astype(jnp.int32)
    far_boxes = draw_far_boxes(jax.random.fold_in(streams_of[6], 71), 0)
    offsets = with_ends(jax.random.randint(streams_of[4], (PARENTS, NI), 0, NOFF), jax.random.fold_in(streams_of[4], 1), 0, NOFF - 1).astype(jnp.int32)
    translation = normal_values(streams_of[5], (NOFF, 2, NT2, NP2), 0.07, 0.5, ((2, 16),), jnp.float32)
    return {"child_patterns": child_patterns, "octants": octants, "parent_map": parent_map, "far_boxes": far_boxes, "offsets": offsets, "translation": translation}


phase_scale = 12.0


def lagrange_table(n_old, n_new, periodic):
    rows = jnp.arange(n_new, dtype=jnp.int32)
    if periodic:
        numer = rows * n_old
        denom = n_new
    else:
        numer = (2 * rows + 1) * n_old - n_new
        denom = 2 * n_new
    start = numer // denom - 2
    if not periodic:
        start = jnp.clip(start, 0, n_old - 6)
    position = numer.astype(jnp.float32) / float(denom) - start.astype(jnp.float32)
    columns = jnp.arange(n_old, dtype=jnp.int32)
    table = jnp.zeros((n_new, n_old), jnp.float32)
    for node in range(6):
        weight = jnp.ones((n_new,), jnp.float32)
        for other in range(6):
            if other != node:
                weight = weight * (position - float(other)) / float(node - other)
        target = start + node
        if periodic:
            target = target % n_old
        table = table + weight[:, None] * (target[:, None] == columns[None, :]).astype(jnp.float32)
    return table


def phase_tables(octants, n_theta, n_phi):
    theta = (jnp.arange(n_theta, dtype=jnp.float32) + 0.5) * (math.pi / n_theta)
    phi = jnp.arange(n_phi, dtype=jnp.float32) * (2.0 * math.pi / n_phi)
    sign_x = (1 - 2 * (octants % 2)).astype(jnp.float32)
    sign_y = (1 - 2 * ((octants // 2) % 2)).astype(jnp.float32)
    sign_z = (1 - 2 * (octants // 4)).astype(jnp.float32)
    along_x = jnp.sin(theta)[:, None] * jnp.cos(phi)[None, :]
    along_y = jnp.sin(theta)[:, None] * jnp.sin(phi)[None, :]
    along_z = jnp.cos(theta)[:, None] * jnp.ones((n_phi,), jnp.float32)[None, :]
    angle = phase_scale * (sign_x[:, None, None] * along_x + sign_y[:, None, None] * along_y + sign_z[:, None, None] * along_z)
    return jnp.cos(angle), jnp.sin(angle)


def aggregate(children, octants, theta_table, phi_table):
    along_phi = jnp.einsum('cktp,qp->cktq', children, phi_table, precision=lax.Precision.HIGHEST)
    fine = jnp.einsum('rt,cktq->ckrq', theta_table, along_phi, precision=lax.Precision.HIGHEST)
    cos_part, sin_part = phase_tables(octants, theta_table.shape[0], phi_table.shape[0])
    real = cos_part * fine[:, 0] - sin_part * fine[:, 1]
    imag = sin_part * fine[:, 0] + cos_part * fine[:, 1]
    return jnp.stack([real, imag], axis=1)


def reference(child_patterns, octants, parent_map, far_boxes, offsets, translation):
    n_theta, n_phi = translation.shape[2], translation.shape[3]
    theta_table = lagrange_table(child_patterns.shape[2], n_theta, False)
    phi_table = lagrange_table(child_patterns.shape[3], n_phi, True)

    def one_group(group_index):
        kids = lax.dynamic_slice_in_dim(child_patterns, group_index * CHILD_GRP, CHILD_GRP, 0)
        kinds = lax.dynamic_slice_in_dim(octants, group_index * CHILD_GRP, CHILD_GRP, 0)
        shifted = aggregate(kids, kinds, theta_table, phi_table)
        owners = parent_map[group_index]
        select = (owners[None, :] == jnp.arange(PAR_GRP, dtype=jnp.int32)[:, None]).astype(jnp.float32)
        summed = jnp.dot(select, shifted.reshape(CHILD_GRP, -1), precision=lax.Precision.HIGHEST)
        return summed.reshape(PAR_GRP, 2, n_theta, n_phi)

    outgoing = lax.map(one_group, jnp.arange(N_BOX, dtype=jnp.int32)).reshape(PARENTS, 2, n_theta, n_phi)
    flat = outgoing.reshape(PARENTS, 2, -1)
    table = translation.reshape(NOFF, 2, -1)

    def step(total, column):
        source = jnp.take(flat, far_boxes[:, column], axis=0)
        factor = jnp.take(table, offsets[:, column], axis=0)
        real = factor[:, 0] * source[:, 0] - factor[:, 1] * source[:, 1]
        imag = factor[:, 0] * source[:, 1] + factor[:, 1] * source[:, 0]
        return total + jnp.stack([real, imag], axis=1), None

    start_total = jnp.zeros(flat.shape, jnp.float32)
    incoming, _ = lax.scan(step, start_total, jnp.arange(NI, dtype=jnp.int32))
    return outgoing, incoming.reshape(PARENTS, 2, n_theta, n_phi)
```

```python
import functools
import math

import jax
import jax.numpy as jnp
import numpy as np
from jax import lax
from jax.experimental import pallas as pl
from jax.experimental.pallas import tpu as pltpu
from jax.sharding import PartitionSpec as P

phase_scale = 12.0
VMEM_LIMIT = 24 * 1024 * 1024


def lagrange_table(n_old, n_new, periodic):
    rows = np.arange(n_new)
    if periodic:
        numer, denom = rows * n_old, n_new
    else:
        numer, denom = (2 * rows + 1) * n_old - n_new, 2 * n_new
    start = numer // denom - 2
    if not periodic:
        start = np.clip(start, 0, n_old - 6)
    position = numer / denom - start
    table = np.zeros((n_new, n_old))
    for node in range(6):
        weight = np.ones(n_new)
        for other in range(6):
            if other != node:
                weight = weight * (position - other) / (node - other)
        target = start + node
        if periodic:
            target = target % n_old
        table[rows, target] += weight
    return table


def high_low(table):
    table = table.astype(np.float32)
    high = table.astype(jnp.bfloat16)
    low = (table - high.astype(np.float32)).astype(jnp.bfloat16)
    return high, low


def split(x):
    high = x.astype(jnp.bfloat16)
    low = (x - high.astype(jnp.float32)).astype(jnp.bfloat16)
    return high, low


def dot3(a, b):
    f = functools.partial(jnp.dot, preferred_element_type=jnp.float32)
    return f(a[0], b[0]) + (f(a[0], b[1]) + f(a[1], b[0]))


def theta_kernel(octants, table_high, table_low, child, out, token, tables, kids, bands, sems):
    n_kids, n_samp = child.shape[0], out.shape[0]
    loads = [pltpu.make_async_copy(child.at[c], kids.at[c], sems.at[c]) for c in range(n_kids)]
    loads[0].start()
    parts = [
        pltpu.make_async_copy(table, tables.at[i], sems.at[n_kids + i])
        for i, table in enumerate((table_high, table_low))
    ]
    for copy in parts:
        copy.start()
    for copy in loads[1:]:
        copy.start()
    row = lax.broadcasted_iota(jnp.int32, (8, out.shape[2]), 0)
    v = jnp.zeros((8, out.shape[2]), jnp.int32)
    for i in range(8):
        v = jnp.where(row == i, octants[i], v)
    v = v.astype(jnp.float32)
    for s in range(n_samp):
        bands[s, 192:200, :] = v
    token[...] = v[:, 0:128]
    for copy in parts:
        copy.wait()
    stores = []
    for c in range(n_kids):
        loads[c].wait()
        x = split(kids[c].reshape(kids.shape[1] * kids.shape[2], kids.shape[3]))
        y = dot3((tables[0], tables[1]), x)
        for s in range(n_samp):
            bands[s, 24 * c : 24 * c + 24, :] = y[24 * s : 24 * s + 24]
        if c % 2:
            first, last = 24 * (c - 1), 24 * (c + 1) + (8 if c == n_kids - 1 else 0)
            rows = pl.ds(first, last - first)
            stores.append(pltpu.make_async_copy(bands.at[:, rows], out.at[:, rows], sems.at[n_kids + 2 + c // 2]))
            stores[-1].start()
    for copy in stores:
        copy.wait()


def prepare_kernel(box, token, table, high, low, cos, sin, out, high_out, low_out, cos_out, sin_out, raw, sems):
    me = box[0]
    n_off = table.shape[0]
    pair, half = me // 2, me % 2
    copies = []
    for q in range(5):
        at = 4 * me + q if q < 4 else 32 + pair
        lanes = pl.ds(pl.multiple_of(128 * (at % 3), 128), 128)
        copies.append(
            pltpu.make_async_copy(table.at[:, at // 3, :, lanes], raw.at[:, q], sems.at[q])
        )
        copies[-1].start()
    high_out[...], low_out[...] = high[...], low[...]
    cos_out[...], sin_out[...] = cos[...], sin[...]
    for copy in copies:
        copy.wait()
    left = lax.broadcasted_iota(jnp.int32, (1, 128), 1) < 64
    upper = jnp.full((1, 128), half, jnp.int32) == 1

    def one(i, carry):
        out[i, 0:8] = jnp.concatenate([raw[i, q] for q in range(4)], 0)
        re, im = raw[i, 4, 0:1], raw[i, 4, 1:2]
        x = jnp.where(left, re, pltpu.roll(im, 64, 1))
        y = jnp.where(left, pltpu.roll(re, 64, 1), im)
        out[i, 8:16] = jnp.broadcast_to(jnp.where(upper, y, x), (8, 128))
        return carry

    lax.fori_loop(0, n_off // 4, lambda i, c: [one(4 * i + u, c) for u in range(4)][-1], 0)


def phi_kernel(owners, lists, table_high, table_low, cos_ref, sin_ref, recv, outgoing, send, total, rows_v, send_v, kinds_v, kinds, sems):
    for s in range(16):
        kinds_v[8 * s : 8 * s + 8, :] = recv[s, 192:200, 0:128].astype(jnp.int32)
    copy = pltpu.make_async_copy(kinds_v, kinds, sems.at[0])
    copy.start()
    total[...] = jnp.zeros_like(total)
    for d in range(8):
        send_v[d, 288:320, :] = lists[...]
    copy.wait()

    def source(s, carry):
        fine = dot3(split(recv[s, 0:192, :]), (table_high[...], table_low[...]))
        for c in range(8):
            child = s * 8 + c
            owner, octant = owners[child], kinds[child, 0]
            f = fine[24 * c : 24 * c + 24]
            cos_0, sin_0 = cos_ref[octant, 0:8], sin_ref[octant, 0:8]
            total[owner, 0:8] += cos_0 * f[0:8] - sin_0 * f[8:16]
            total[owner, 8:16] += sin_0 * f[0:8] + cos_0 * f[8:16]
            swapped = pltpu.roll(f[16:24], 4, 0)
            total[owner, 16:24] += cos_ref[octant, 8:16] * f[16:24] + sin_ref[octant, 8:16] * swapped
        return carry

    lax.fori_loop(0, 16, source, 0)

    def parent(p, carry):
        for l in range(3):
            v = total[p, :, 128 * l : 128 * l + 128]
            base = 72 * p + 2 * l
            rows_v[pl.ds(base, 8, stride=6), :] = v[0:8]
            rows_v[pl.ds(base + 1, 8, stride=6), :] = v[8:16]
            rows_v[pl.ds(base + 48, 4, stride=6), :] = v[16:20]
            rows_v[pl.ds(base + 49, 4, stride=6), :] = v[20:24]
        for d in range(8):
            at = pl.multiple_of(72 * p + 8 * d, 8)
            send_v[d, pl.ds(pl.multiple_of(8 * p, 8), 8), :] = rows_v[pl.ds(at, 8), :]
        return carry

    left = lax.broadcasted_iota(jnp.int32, (8, 128), 1) < 64
    copies = []
    for q in range(4):
        lax.fori_loop(8 * q, 8 * q + 8, parent, 0)
        rows = pl.ds(64 * q, 64)
        copies.append(pltpu.make_async_copy(send_v.at[:, rows], send.at[:, rows], sems.at[1 + q]))
        copies[-1].start()
        for r in range(4):
            at = 72 * 8 * q + 64 + 2 * r
            re, im = rows_v[pl.ds(at, 8, stride=72), :], rows_v[pl.ds(at + 1, 8, stride=72), :]
            rows = slice(256 + 8 * q, 264 + 8 * q)
            send_v[2 * r, rows, :] = jnp.where(left, re, pltpu.roll(im, 64, 1))
            send_v[2 * r + 1, rows, :] = jnp.where(left, pltpu.roll(re, 64, 1), im)
    rows = pl.ds(256, 64)
    copies.append(pltpu.make_async_copy(send_v.at[:, rows], send.at[:, rows], sems.at[5]))
    copies[-1].start()
    copies.append(pltpu.make_async_copy(rows_v, outgoing, sems.at[6]))
    copies[-1].start()
    for copy in copies:
        copy.wait()


def translate_kernel(recv, factor, send, source, sums, send_v, idx_v, idx, sems):
    copies = []
    for b in range(8):
        rows = pl.ds(32 * b, 32)
        idx_v[rows, :] = recv[b, 288:320, :].astype(jnp.int32)
        copies.append(pltpu.make_async_copy(idx_v.at[rows], idx.at[rows], sems.at[b]))
        copies[-1].start()
    left = lax.broadcasted_iota(jnp.int32, (8, 128), 1) < 64
    even = lax.broadcasted_iota(jnp.int32, (8, 128), 0) % 2 == 0
    for b in range(8):

        def prepare(p, carry):
            v = recv[b, pl.ds(pl.multiple_of(8 * p, 8), 8), :]
            at = pl.multiple_of((b * 32 + p) * 24, 8)
            source[pl.ds(at, 8), :] = jnp.where(even, v, pltpu.roll(v, 1, 0))
            source[pl.ds(at + 8, 8), :] = jnp.where(even, pltpu.roll(v, 7, 0), v)
            return carry

        lax.fori_loop(0, 32, prepare, 0, unroll=8)
        for q in range(4):
            v = recv[b, 256 + 8 * q : 264 + 8 * q, :]
            r = pltpu.roll(v, 64, 1)
            at = (b * 32 + 8 * q) * 24 + 16
            source[pl.ds(at, 8, stride=24), :] = jnp.where(left, v, r)
            source[pl.ds(at + 1, 8, stride=24), :] = jnp.where(left, r, v)

    n_far = 48

    def one(row, carry):
        acc = [jnp.zeros((8, 128), jnp.float32) for _ in range(3)]
        for j in range(n_far):
            f = pl.multiple_of(idx[row, j], 8)
            o = pl.multiple_of(idx[row, n_far + j], 8)
            t = factor[pl.ds(o, 8), :]
            acc[0] += t * source[pl.ds(f, 8), :]
            acc[1] += t * source[pl.ds(f + 8, 8), :]
            acc[2] += factor[pl.ds(o + 8, 8), :] * source[pl.ds(f + 16, 8), :]
        for k in range(3):
            sums[pl.ds(pl.multiple_of(24 * row, 8) + 8 * k, 8), :] = acc[k]
        return carry

    def finish(p, b):
        at = pl.multiple_of((b * 32 + p) * 24, 8)
        r = sums[pl.ds(at + 8, 8), :]
        r = jnp.where(even, -pltpu.roll(r, 7, 0), pltpu.roll(r, 1, 0))
        send_v[b, pl.ds(pl.multiple_of(8 * p, 8), 8), :] = sums[pl.ds(at, 8), :] + r
        return b

    for copy in copies:
        copy.wait()
    lax.fori_loop(0, 256, one, 0)
    copies = []
    for b in range(8):
        lax.fori_loop(0, 32, finish, b, unroll=8)
        for q in range(4):
            at = (b * 32 + 8 * q) * 24 + 16
            r = pltpu.roll(sums[pl.ds(at + 1, 8, stride=24), :], 64, 1)
            rows = slice(256 + 8 * q, 264 + 8 * q)
            send_v[b, rows, :] = sums[pl.ds(at, 8, stride=24), :] + jnp.where(left, -r, r)
        if b % 2:
            two = pl.ds(b - 1, 2)
            copies.append(pltpu.make_async_copy(send_v.at[two], send.at[two], sems.at[8 + b // 2]))
            copies[-1].start()
    for copy in copies:
        copy.wait()


def place_rows_kernel(rows, out):
    def one(p, carry):
        for at in range(36):
            v = rows[pl.ds(pl.multiple_of(72 * p, 8) + 2 * at, 2), :]
            out[p, at // 3, :, 128 * (at % 3) : 128 * (at % 3) + 128] = v
        return carry

    lax.fori_loop(0, 32, one, 0)


def place_kernel(recv, out, last):
    left = lax.broadcasted_iota(jnp.int32, (8, 128), 1) < 64
    for q in range(4):
        for r in range(4):
            rows = slice(256 + 8 * q, 264 + 8 * q)
            e, o = recv[2 * r, rows, :], recv[2 * r + 1, rows, :]
            at = 8 * 8 * q + 2 * r
            last[pl.ds(at, 8, stride=8), :] = jnp.where(left, e, pltpu.roll(o, 64, 1))
            last[pl.ds(at + 1, 8, stride=8), :] = jnp.where(left, pltpu.roll(e, 64, 1), o)

    def one(p, carry):
        base = pl.multiple_of(8 * p, 8)
        for at in range(36):
            rows = pl.ds(base + 2 * (at % 4), 2)
            v = recv[at // 4, rows, :] if at < 32 else last[rows, :]
            out[p, at // 3, :, 128 * (at % 3) : 128 * (at % 3) + 128] = v
        return carry

    lax.fori_loop(0, 32, one, 0)


def phase_tables(samp, n_theta, n_phi):
    polar = np.concatenate([np.arange(12), np.arange(8, 12)])
    sign = np.where((np.arange(16) >= 8) & (np.arange(16) < 12), -1.0, 1.0).astype(np.float32)
    theta = (samp * 12 + polar).astype(jnp.float32) * (math.pi / n_theta) + 0.5 * math.pi / n_theta
    phi = np.arange(n_phi) * (2.0 * math.pi / n_phi)
    o = np.arange(8)
    sx, sy, sz = 1.0 - 2 * (o % 2), 1.0 - 2 * (o // 2 % 2), 1.0 - 2 * (o // 4)
    around = (sx[:, None] * np.cos(phi) + sy[:, None] * np.sin(phi)).astype(np.float32)
    angle = phase_scale * (
        jnp.sin(theta)[None, :, None] * around[:, None, :]
        + (sz.astype(np.float32)[:, None] * jnp.cos(theta)[None, :])[:, :, None]
    )
    return jnp.cos(angle), jnp.sin(angle) * sign[None, :, None]


def vmem():
    return pl.BlockSpec(memory_space=pltpu.VMEM)


def smem():
    return pl.BlockSpec(memory_space=pltpu.SMEM)


def held(x):
    return pltpu.with_memory_space_constraint(x, pltpu.VMEM)


def params():
    return pltpu.CompilerParams(vmem_limit_bytes=VMEM_LIMIT)


def anywhere():
    return pl.BlockSpec(memory_space=pl.ANY)


def far_away(x):
    return pltpu.with_memory_space_constraint(x, pltpu.HBM)


def shards(child_patterns, octants, parent_map, far_boxes, offsets, translation):
    n_box, n_samp = lax.axis_size("box"), lax.axis_size("samp")
    count, _, n_t1, n_p1 = child_patterns.shape
    n_off, _, band, n_p2 = translation.shape
    n_t2 = band * n_samp
    parents, n_far = far_boxes.shape
    box, samp = lax.axis_index("box"), lax.axis_index("samp")
    f32, bf16 = jnp.float32, jnp.bfloat16

    theta_table = lagrange_table(n_t1, n_t2, False).reshape(n_samp, band, n_t1)
    both = np.zeros((n_samp, 24, 2, n_t1))
    both[:, 0:8, 0], both[:, 8:16, 1] = theta_table[:, 0:8], theta_table[:, 0:8]
    both[:, 16:20, 0], both[:, 20:24, 1] = theta_table[:, 8:12], theta_table[:, 8:12]
    theta_high, theta_low = high_low(both.reshape(n_samp * 24, 2 * n_t1))
    phi_high, phi_low = high_low(lagrange_table(n_p1, n_p2, True).T)

    sent = (n_samp, 24 * count + 8, n_p1)
    bands, token = pl.pallas_call(
        theta_kernel,
        in_specs=[smem()] + [anywhere()] * 3,
        out_specs=[anywhere(), vmem()],
        out_shape=[pltpu.HBM(sent, f32), jax.ShapeDtypeStruct((8, 128), f32)],
        scratch_shapes=[
            pltpu.VMEM((2, n_samp * 24, 2 * n_t1), bf16),
            pltpu.VMEM(child_patterns.shape, f32),
            pltpu.VMEM(sent, f32),
            pltpu.SemaphoreType.DMA((count + 2 + count // 2,)),
        ],
        compiler_params=params(),
        name="theta",
    )(octants, far_away(theta_high), far_away(theta_low), far_away(child_patterns))
    bands = lax.all_to_all(bands, "samp", 0, 0)

    cos_part, sin_part = phase_tables(samp, n_t2, n_p2)
    factor, *tables = pl.pallas_call(
        prepare_kernel,
        in_specs=[smem(), vmem(), anywhere()] + [vmem()] * 4,
        out_specs=[vmem()] * 5,
        out_shape=[
            pltpu.VMEM((n_off, 16, 128), f32),
            pltpu.VMEM(phi_high.shape, bf16),
            pltpu.VMEM(phi_high.shape, bf16),
            pltpu.VMEM(cos_part.shape, f32),
            pltpu.VMEM(cos_part.shape, f32),
        ],
        scratch_shapes=[pltpu.VMEM((n_off, 5, 2, 128), f32), pltpu.SemaphoreType.DMA((5,))],
        compiler_params=params(),
        cost_estimate=pl.CostEstimate(flops=10**7, bytes_accessed=10**7, transcendentals=0),
        name="prepare",
    )(box.reshape(1), token, far_away(translation.transpose(0, 2, 1, 3)), phi_high, phi_low, cos_part, sin_part)
    lists = jnp.concatenate([far_boxes * 24, offsets * 16, jnp.zeros((parents, 128 - 2 * n_far), jnp.int32)], 1)

    outgoing, send = pl.pallas_call(
        phi_kernel,
        in_specs=[smem()] + [vmem()] * 6,
        out_specs=[anywhere()] * 2,
        out_shape=[pltpu.HBM((parents * 72, 128), f32), pltpu.HBM((n_box, 10 * parents, 128), f32)],
        scratch_shapes=[
            pltpu.VMEM((parents, 24, n_p2), f32),
            pltpu.VMEM((parents * 72, 128), f32),
            pltpu.VMEM((n_box, 10 * parents, 128), f32),
            pltpu.VMEM((n_samp * count, 128), jnp.int32),
            pltpu.SMEM((n_samp * count, 128), jnp.int32),
            pltpu.SemaphoreType.DMA((7,)),
        ],
        compiler_params=params(),
        name="phi",
    )(parent_map[0], lists.astype(f32), *[held(x) for x in tables], held(bands))

    everywhere = lax.all_to_all(send, "box", 0, 0)
    n_all = n_box * parents
    back = pl.pallas_call(
        translate_kernel,
        in_specs=[vmem(), vmem()],
        out_specs=anywhere(),
        out_shape=pltpu.HBM((n_box, 9 * parents, 128), f32),
        scratch_shapes=[
            pltpu.VMEM((n_all * 24, 128), f32),
            pltpu.VMEM((n_all * 24, 128), f32),
            pltpu.VMEM((n_box, 9 * parents, 128), f32),
            pltpu.VMEM((n_all, 128), jnp.int32),
            pltpu.SMEM((n_all, 128), jnp.int32),
            pltpu.SemaphoreType.DMA((12,)),
        ],
        compiler_params=params(),
        name="translate",
    )(held(everywhere), held(factor.reshape(n_off * 16, 128)))
    back = lax.all_to_all(back, "box", 0, 0)
    shape = jax.ShapeDtypeStruct((parents, band, 2, n_p2), f32)
    outgoing = pl.pallas_call(
        place_rows_kernel,
        in_specs=[vmem()],
        out_specs=vmem(),
        out_shape=shape,
        compiler_params=params(),
        cost_estimate=pl.CostEstimate(flops=10**6, bytes_accessed=4 * 10**6, transcendentals=0),
        name="place_rows",
    )(outgoing)
    incoming = pl.pallas_call(
        place_kernel,
        in_specs=[vmem()],
        out_specs=vmem(),
        out_shape=shape,
        scratch_shapes=[pltpu.VMEM((8 * parents, 128), f32)],
        compiler_params=params(),
        name="place",
    )(held(back))
    return outgoing.transpose(0, 2, 1, 3), incoming.transpose(0, 2, 1, 3)


def solution(mesh):
    in_specs = (
        P(("box", "samp"), None, None, None),
        P(("box", "samp")),
        P("box", None),
        P("box", None),
        P("box", None),
        P(None, None, "samp", None),
    )
    out_specs = (P("box", None, "samp", None), P("box", None, "samp", None))
    return jax.shard_map(shards, mesh=mesh, in_specs=in_specs, out_specs=out_specs, check_vma=False)
```

```python
import functools
import math

import jax
import jax.numpy as jnp
import numpy as np
from jax import lax
from jax.experimental import pallas as pl
from jax.experimental.pallas import tpu as pltpu
from jax.sharding import PartitionSpec as P

phase_scale = 12.0
VMEM_LIMIT = 24 * 1024 * 1024


def lagrange_table(n_old, n_new, periodic):
    rows = np.arange(n_new)
    if periodic:
        numer, denom = rows * n_old, n_new
    else:
        numer, denom = (2 * rows + 1) * n_old - n_new, 2 * n_new
    start = numer // denom - 2
    if not periodic:
        start = np.clip(start, 0, n_old - 6)
    position = numer / denom - start
    table = np.zeros((n_new, n_old))
    for node in range(6):
        weight = np.ones(n_new)
        for other in range(6):
            if other != node:
                weight = weight * (position - other) / (node - other)
        target = start + node
        if periodic:
            target = target % n_old
        table[rows, target] += weight
    return table


def high_low(table):
    table = table.astype(np.float32)
    high = table.astype(jnp.bfloat16)
    low = (table - high.astype(np.float32)).astype(jnp.bfloat16)
    return high, low


def split(x):
    high = x.astype(jnp.bfloat16)
    low = (x - high.astype(jnp.float32)).astype(jnp.bfloat16)
    return high, low


def dot3(a, b):
    f = functools.partial(jnp.dot, preferred_element_type=jnp.float32)
    return f(a[0], b[0]) + (f(a[0], b[1]) + f(a[1], b[0]))


def theta_kernel(octants, table_high, table_low, child, out, token, tables, kids, bands, kinds, sems):
    n_kids, n_samp = child.shape[0], out.shape[0]
    loads = [pltpu.make_async_copy(child.at[c], kids.at[c], sems.at[c]) for c in range(n_kids)]
    loads[0].start()
    parts = [
        pltpu.make_async_copy(table, tables.at[i], sems.at[n_kids + i])
        for i, table in enumerate((table_high, table_low))
    ]
    for copy in parts:
        copy.start()
    small = pltpu.make_async_copy(octants, kinds, sems.at[n_kids + 2])
    small.start()
    for copy in loads[1:]:
        copy.start()
    small.wait()
    row = lax.broadcasted_iota(jnp.int32, (8, 128), 0)
    v = jnp.zeros((8, 128), jnp.int32)
    for i in range(8):
        v = jnp.where(row == i, kinds[0, i], v)
    v = v.astype(jnp.float32)
    for s in range(n_samp):
        bands[s, 384:392, :] = v
    token[...] = v
    stores = []

    def store(first, count):
        rows = pl.ds(first, count)
        stores.append(pltpu.make_async_copy(bands.at[:, rows], out.at[:, rows], sems.at[n_kids + 3 + len(stores)]))
        stores[-1].start()

    for copy in parts:
        copy.wait()
    for c in range(n_kids):
        loads[c].wait()
        x = split(kids[c].reshape(kids.shape[1] * kids.shape[2], kids.shape[3]))
        y = dot3((tables[0], tables[1]), x)
        for s in range(n_samp):
            bands[s, 24 * c : 24 * c + 24, :] = y[24 * s : 24 * s + 24, 0:128]
            bands[s, 192 + 24 * c : 216 + 24 * c, :] = y[24 * s : 24 * s + 24, 128:256]
        if c % 2:
            store(24 * (c - 1), 48)
            store(192 + 24 * (c - 1), 48 + 8 * (c == n_kids - 1))
    for copy in stores:
        copy.wait()


def prepare_kernel(box, token, table, out, done, raw, sems):
    me = box[0]
    n_off = table.shape[0]
    pair, half = me // 2, me % 2
    copies = []
    for q in range(5):
        at = 4 * me + q if q < 4 else 32 + pair
        lanes = pl.ds(pl.multiple_of(128 * (at % 3), 128), 128)
        copies.append(
            pltpu.make_async_copy(table.at[:, at // 3, :, lanes], raw.at[:, q], sems.at[q])
        )
        copies[-1].start()
    done[...] = token[...]
    for copy in copies:
        copy.wait()
    left = lax.broadcasted_iota(jnp.int32, (1, 128), 1) < 64
    upper = jnp.full((1, 128), half, jnp.int32) == 1

    def one(i, carry):
        out[i, 0:8] = jnp.concatenate([raw[i, q] for q in range(4)], 0)
        re, im = raw[i, 4, 0:1], raw[i, 4, 1:2]
        x = jnp.where(left, re, pltpu.roll(im, 64, 1))
        y = jnp.where(left, pltpu.roll(re, 64, 1), im)
        out[i, 8:16] = jnp.broadcast_to(jnp.where(upper, y, x), (8, 128))
        return carry

    lax.fori_loop(0, n_off // 4, lambda i, c: [one(4 * i + u, c) for u in range(4)][-1], 0)


def phi_kernel(
    owners, token, lists, table_high, table_low, cos_hbm, sin_hbm, recv, outgoing, send,
    total, fine, rows_v, send_v, tables, cos_ref, sin_ref, kinds_v, kinds, sems,
):
    pairs = [(table_high, tables.at[0]), (table_low, tables.at[1]), (cos_hbm, cos_ref), (sin_hbm, sin_ref)]
    loads = [pltpu.make_async_copy(a, b, sems.at[i]) for i, (a, b) in enumerate(pairs)]
    for copy in loads:
        copy.start()
    for s in range(16):
        kinds_v[8 * s : 8 * s + 8, :] = recv[s, 384:392, :].astype(jnp.int32)
    copy = pltpu.make_async_copy(kinds_v, kinds, sems.at[4])
    copy.start()
    total[...] = jnp.zeros_like(total)
    for d in range(8):
        send_v[d, 288:312, :] = lists[...]
    for load in loads[:2]:
        load.wait()
    table = jnp.concatenate([tables[0], tables[0], tables[1]], 0)

    def product(s):
        high, low = split(jnp.concatenate([recv[s, 0:192, :], recv[s, 192:384, :]], 1))
        return jnp.dot(jnp.concatenate([high, low, high], 1), table, preferred_element_type=jnp.float32)

    def add(s, fine):
        for c in range(8):
            child = s * 8 + c
            owner, octant = owners[child], kinds[child, 0]
            f = fine[24 * c : 24 * c + 24, :]
            cos_0, sin_0 = cos_ref[octant, 0:8], sin_ref[octant, 0:8]
            total[owner, 0:8] += cos_0 * f[0:8] - sin_0 * f[8:16]
            total[owner, 8:16] += sin_0 * f[0:8] + cos_0 * f[8:16]
            swapped = pltpu.roll(f[16:24], 4, 0)
            total[owner, 16:24] += cos_ref[octant, 8:16] * f[16:24] + sin_ref[octant, 8:16] * swapped

    fine[0] = product(0)
    for load in loads[2:]:
        load.wait()
    copy.wait()

    def two(i, carry):
        s = 2 * i
        fine[1] = product(s + 1)
        add(s, fine.at[0])
        fine[0] = product(lax.rem(s + 2, 16))
        add(s + 1, fine.at[1])
        return carry

    lax.fori_loop(0, 8, two, 0, unroll=2)

    def parent(p, carry):
        for l in range(3):
            v = total[p, :, 128 * l : 128 * l + 128]
            base = 72 * p + 2 * l
            rows_v[pl.ds(base, 8, stride=6), :] = v[0:8]
            rows_v[pl.ds(base + 1, 8, stride=6), :] = v[8:16]
            rows_v[pl.ds(base + 48, 4, stride=6), :] = v[16:20]
            rows_v[pl.ds(base + 49, 4, stride=6), :] = v[20:24]
        for d in range(8):
            at = pl.multiple_of(72 * p + 8 * d, 8)
            send_v[d, pl.ds(pl.multiple_of(8 * p, 8), 8), :] = rows_v[pl.ds(at, 8), :]
        return carry

    left = lax.broadcasted_iota(jnp.int32, (8, 128), 1) < 64
    copies = []
    for q in range(4):
        lax.fori_loop(8 * q, 8 * q + 8, parent, 0)
        rows = pl.ds(64 * q, 64)
        copies.append(pltpu.make_async_copy(send_v.at[:, rows], send.at[:, rows], sems.at[5 + q]))
        copies[-1].start()
        rows = pl.ds(576 * q, 576)
        copies.append(pltpu.make_async_copy(rows_v.at[rows], outgoing.at[rows], sems.at[9 + q]))
        copies[-1].start()
        for r in range(4):
            at = 72 * 8 * q + 64 + 2 * r
            re, im = rows_v[pl.ds(at, 8, stride=72), :], rows_v[pl.ds(at + 1, 8, stride=72), :]
            rows = slice(256 + 8 * q, 264 + 8 * q)
            send_v[2 * r, rows, :] = jnp.where(left, re, pltpu.roll(im, 64, 1))
            send_v[2 * r + 1, rows, :] = jnp.where(left, pltpu.roll(re, 64, 1), im)
    rows = pl.ds(256, 56)
    copies.append(pltpu.make_async_copy(send_v.at[:, rows], send.at[:, rows], sems.at[13]))
    copies[-1].start()
    for copy in copies:
        copy.wait()


def translate_kernel(recv, factor, send, source, sums, send_v, idx_v, idx, load_sems, store_sems):
    n_far, n_own = 48, 32
    loads = []
    for b in range(8):
        rows = pl.ds(24 * b, 24)
        idx_v[rows, :] = recv[b, 288:312, :].astype(jnp.int32)
        loads.append(pltpu.make_async_copy(idx_v.at[rows], idx.at[rows], load_sems.at[b]))
        loads[-1].start()
    left = lax.broadcasted_iota(jnp.int32, (8, 128), 1) < 64
    even = lax.broadcasted_iota(jnp.int32, (8, 128), 0) % 2 == 0
    for b in range(8):

        def prepare(p, carry):
            v = recv[b, pl.ds(pl.multiple_of(8 * p, 8), 8), :]
            at = pl.multiple_of((b * n_own + p) * 24, 8)
            source[pl.ds(at, 8), :] = jnp.where(even, v, pltpu.roll(v, 1, 0))
            source[pl.ds(at + 8, 8), :] = jnp.where(even, pltpu.roll(v, 7, 0), v)
            return carry

        lax.fori_loop(0, n_own, prepare, 0, unroll=8)
        for q in range(4):
            v = recv[b, 256 + 8 * q : 264 + 8 * q, :]
            r = pltpu.roll(v, 64, 1)
            at = (b * n_own + 8 * q) * 24 + 16
            source[pl.ds(at, 8, stride=24), :] = jnp.where(left, v, r)
            source[pl.ds(at + 1, 8, stride=24), :] = jnp.where(left, r, v)

    def index(j, b, p):
        return pl.multiple_of(idx.at[pl.ds(j // 4, 169), pl.ds(n_own * (j % 4), n_own)][24 * b, p], 8)

    def some(i, b):
        acc = [[jnp.zeros((8, 128), jnp.float32) for _ in range(3)] for _ in range(4)]
        for j in range(n_far):
            for h in range(4):
                f, o = index(j, b, 4 * i + h), index(n_far + j, b, 4 * i + h)
                t = factor[pl.ds(o, 8), :]
                acc[h][0] += t * source[pl.ds(f, 8), :]
                acc[h][1] += t * source[pl.ds(f + 8, 8), :]
                acc[h][2] += factor[pl.ds(o + 8, 8), :] * source[pl.ds(f + 16, 8), :]
        for h in range(4):
            for k in range(3):
                sums[pl.ds(pl.multiple_of(24 * (b * n_own + 4 * i), 8) + 24 * h + 8 * k, 8), :] = acc[h][k]
        return b

    def finish(p, b):
        at = pl.multiple_of((b * n_own + p) * 24, 8)
        r = sums[pl.ds(at + 8, 8), :]
        r = jnp.where(even, -pltpu.roll(r, 7, 0), pltpu.roll(r, 1, 0))
        send_v[b, pl.ds(pl.multiple_of(8 * p, 8), 8), :] = sums[pl.ds(at, 8), :] + r
        return b

    def store(b):
        return pltpu.make_async_copy(send_v.at[pl.ds(b, 1)], send.at[pl.ds(b, 1)], store_sems.at[b])

    def box(b, carry):
        rows = pl.ds(pl.multiple_of(24 * b, 8), 24)
        pltpu.make_async_copy(idx_v.at[rows], idx.at[rows], load_sems.at[b]).wait()
        lax.fori_loop(0, n_own // 4, some, b)
        lax.fori_loop(0, n_own, finish, b, unroll=8)
        for q in range(4):
            at = (b * n_own + 8 * q) * 24 + 16
            r = pltpu.roll(sums[pl.ds(at + 1, 8, stride=24), :], 64, 1)
            rows = slice(256 + 8 * q, 264 + 8 * q)
            send_v[b, rows, :] = sums[pl.ds(at, 8, stride=24), :] + jnp.where(left, -r, r)
        store(b).start()
        return carry

    lax.fori_loop(0, 8, box, 0)
    for b in range(8):
        store(b).wait()


def place_rows_kernel(rows, out):
    def one(p, carry):
        for at in range(36):
            v = rows[pl.ds(pl.multiple_of(72 * p, 8) + 2 * at, 2), :]
            out[p, at // 3, :, 128 * (at % 3) : 128 * (at % 3) + 128] = v
        return carry

    lax.fori_loop(0, 32, one, 0)


def place_kernel(recv, out, last):
    left = lax.broadcasted_iota(jnp.int32, (8, 128), 1) < 64
    for q in range(4):
        for r in range(4):
            rows = slice(256 + 8 * q, 264 + 8 * q)
            e, o = recv[2 * r, rows, :], recv[2 * r + 1, rows, :]
            at = 8 * 8 * q + 2 * r
            last[pl.ds(at, 8, stride=8), :] = jnp.where(left, e, pltpu.roll(o, 64, 1))
            last[pl.ds(at + 1, 8, stride=8), :] = jnp.where(left, pltpu.roll(e, 64, 1), o)

    def one(p, carry):
        base = pl.multiple_of(8 * p, 8)
        for at in range(36):
            rows = pl.ds(base + 2 * (at % 4), 2)
            v = recv[at // 4, rows, :] if at < 32 else last[rows, :]
            out[p, at // 3, :, 128 * (at % 3) : 128 * (at % 3) + 128] = v
        return carry

    lax.fori_loop(0, 32, one, 0)


def phase_tables(samp, n_theta, n_phi):
    polar = np.concatenate([np.arange(12), np.arange(8, 12)])
    sign = np.where((np.arange(16) >= 8) & (np.arange(16) < 12), -1.0, 1.0).astype(np.float32)
    theta = (samp * 12 + polar).astype(jnp.float32) * (math.pi / n_theta) + 0.5 * math.pi / n_theta
    phi = np.arange(n_phi) * (2.0 * math.pi / n_phi)
    o = np.arange(8)
    sx, sy, sz = 1.0 - 2 * (o % 2), 1.0 - 2 * (o // 2 % 2), 1.0 - 2 * (o // 4)
    around = (sx[:, None] * np.cos(phi) + sy[:, None] * np.sin(phi)).astype(np.float32)
    angle = phase_scale * (
        jnp.sin(theta)[None, :, None] * around[:, None, :]
        + (sz.astype(np.float32)[:, None] * jnp.cos(theta)[None, :])[:, :, None]
    )
    return jnp.cos(angle), jnp.sin(angle) * sign[None, :, None]


def vmem():
    return pl.BlockSpec(memory_space=pltpu.VMEM)


def smem():
    return pl.BlockSpec(memory_space=pltpu.SMEM)


def held(x):
    return pltpu.with_memory_space_constraint(x, pltpu.VMEM)


def params():
    return pltpu.CompilerParams(vmem_limit_bytes=VMEM_LIMIT)


def anywhere():
    return pl.BlockSpec(memory_space=pl.ANY)


def far_away(x):
    return pltpu.with_memory_space_constraint(x, pltpu.HBM)


def shards(child_patterns, octants, parent_map, far_boxes, offsets, translation):
    n_box, n_samp = lax.axis_size("box"), lax.axis_size("samp")
    count, _, n_t1, n_p1 = child_patterns.shape
    n_off, _, band, n_p2 = translation.shape
    n_t2 = band * n_samp
    parents, n_far = far_boxes.shape
    box, samp = lax.axis_index("box"), lax.axis_index("samp")
    f32, bf16 = jnp.float32, jnp.bfloat16

    theta_table = lagrange_table(n_t1, n_t2, False).reshape(n_samp, band, n_t1)
    both = np.zeros((n_samp, 24, 2, n_t1))
    both[:, 0:8, 0], both[:, 8:16, 1] = theta_table[:, 0:8], theta_table[:, 0:8]
    both[:, 16:20, 0], both[:, 20:24, 1] = theta_table[:, 8:12], theta_table[:, 8:12]
    theta_high, theta_low = high_low(both.reshape(n_samp * 24, 2 * n_t1))
    phi_high, phi_low = high_low(lagrange_table(n_p1, n_p2, True).T)

    sent = (n_samp, 48 * count + 8, 128)
    bands, token = pl.pallas_call(
        theta_kernel,
        in_specs=[anywhere()] * 4,
        out_specs=[anywhere(), vmem()],
        out_shape=[pltpu.HBM(sent, f32), jax.ShapeDtypeStruct((8, 128), f32)],
        scratch_shapes=[
            pltpu.VMEM((2, n_samp * 24, 2 * n_t1), bf16),
            pltpu.VMEM(child_patterns.shape, f32),
            pltpu.VMEM(sent, f32),
            pltpu.SMEM((1, count), jnp.int32),
            pltpu.SemaphoreType.DMA((2 * count + 3,)),
        ],
        compiler_params=params(),
        name="theta",
    )(far_away(octants.reshape(1, count)), far_away(theta_high), far_away(theta_low), far_away(child_patterns))
    bands = lax.all_to_all(bands, "samp", 0, 0)

    cos_part, sin_part = phase_tables(samp, n_t2, n_p2)
    factor, token = pl.pallas_call(
        prepare_kernel,
        in_specs=[smem(), vmem(), anywhere()],
        out_specs=[vmem()] * 2,
        out_shape=[pltpu.VMEM((n_off, 16, 128), f32), jax.ShapeDtypeStruct((8, 128), f32)],
        scratch_shapes=[pltpu.VMEM((n_off, 5, 2, 128), f32), pltpu.SemaphoreType.DMA((5,))],
        compiler_params=params(),
        cost_estimate=pl.CostEstimate(flops=10**7, bytes_accessed=10**7, transcendentals=0),
        name="prepare",
    )(box.reshape(1), token, far_away(translation.transpose(0, 2, 1, 3)))
    lists = jnp.concatenate([far_boxes.T * 24, offsets.T * 16], 0).reshape(24, 128)

    outgoing, send = pl.pallas_call(
        phi_kernel,
        in_specs=[smem(), vmem(), vmem()] + [anywhere()] * 4 + [vmem()],
        out_specs=[anywhere()] * 2,
        out_shape=[pltpu.HBM((parents * 72, 128), f32), pltpu.HBM((n_box, 9 * parents + 24, 128), f32)],
        scratch_shapes=[
            pltpu.VMEM((parents, 24, n_p2), f32),
            pltpu.VMEM((2, 24 * count, n_p2), f32),
            pltpu.VMEM((parents * 72, 128), f32),
            pltpu.VMEM((n_box, 9 * parents + 24, 128), f32),
            pltpu.VMEM((2, n_p1, n_p2), bf16),
            pltpu.VMEM(cos_part.shape, f32),
            pltpu.VMEM(cos_part.shape, f32),
            pltpu.VMEM((n_samp * count, 128), jnp.int32),
            pltpu.SMEM((n_samp * count, 128), jnp.int32),
            pltpu.SemaphoreType.DMA((14,)),
        ],
        compiler_params=params(),
        name="phi",
    )(
        parent_map[0], token, lists.astype(f32),
        *[far_away(x) for x in (phi_high, phi_low, cos_part, sin_part)], held(bands),
    )

    everywhere = lax.all_to_all(send, "box", 0, 0)
    n_all = n_box * parents
    back = pl.pallas_call(
        translate_kernel,
        in_specs=[vmem(), vmem()],
        out_specs=anywhere(),
        out_shape=pltpu.HBM((n_box, 9 * parents, 128), f32),
        scratch_shapes=[
            pltpu.VMEM((n_all * 24, 128), f32),
            pltpu.VMEM((n_all * 24, 128), f32),
            pltpu.VMEM((n_box, 9 * parents, 128), f32),
            pltpu.VMEM((24 * n_box, 128), jnp.int32),
            pltpu.SMEM((24 * n_box, 128), jnp.int32),
            pltpu.SemaphoreType.DMA((n_box,)),
            pltpu.SemaphoreType.DMA((n_box,)),
        ],
        compiler_params=params(),
        name="translate",
    )(held(everywhere), held(factor.reshape(n_off * 16, 128)))
    back = lax.all_to_all(back, "box", 0, 0)
    shape = jax.ShapeDtypeStruct((parents, band, 2, n_p2), f32)
    outgoing = pl.pallas_call(
        place_rows_kernel,
        in_specs=[vmem()],
        out_specs=vmem(),
        out_shape=shape,
        compiler_params=params(),
        cost_estimate=pl.CostEstimate(flops=10**6, bytes_accessed=4 * 10**6, transcendentals=0),
        name="place_rows",
    )(outgoing)
    incoming = pl.pallas_call(
        place_kernel,
        in_specs=[vmem()],
        out_specs=vmem(),
        out_shape=shape,
        scratch_shapes=[pltpu.VMEM((8 * parents, 128), f32)],
        compiler_params=params(),
        name="place",
    )(held(back))
    return outgoing.transpose(0, 2, 1, 3), incoming.transpose(0, 2, 1, 3)


def solution(mesh):
    in_specs = (
        P(("box", "samp"), None, None, None),
        P(("box", "samp")),
        P("box", None),
        P("box", None),
        P("box", None),
        P(None, None, "samp", None),
    )
    out_specs = (P("box", None, "samp", None), P("box", None, "samp", None))
    return jax.shard_map(shards, mesh=mesh, in_specs=in_specs, out_specs=out_specs, check_vma=False)
```

```python
import functools
import math

import jax
import jax.numpy as jnp
import numpy as np
from jax import lax
from jax.experimental import pallas as pl
from jax.experimental.pallas import tpu as pltpu
from jax.sharding import PartitionSpec as P

phase_scale = 12.0


def lagrange_table(n_old, n_new, periodic):
    rows = np.arange(n_new)
    if periodic:
        numer, denom = rows * n_old, n_new
    else:
        numer, denom = (2 * rows + 1) * n_old - n_new, 2 * n_new
    start = numer // denom - 2
    if not periodic:
        start = np.clip(start, 0, n_old - 6)
    position = numer / denom - start
    table = np.zeros((n_new, n_old))
    for node in range(6):
        weight = np.ones(n_new)
        for other in range(6):
            if other != node:
                weight = weight * (position - other) / (node - other)
        target = start + node
        if periodic:
            target = target % n_old
        table[rows, target] += weight
    return table


def high_low(table):
    table = table.astype(np.float32)
    high = table.astype(jnp.bfloat16)
    low = (table - high.astype(np.float32)).astype(jnp.bfloat16)
    return high, low


def split(x):
    high = x.astype(jnp.bfloat16)
    low = (x - high.astype(jnp.float32)).astype(jnp.bfloat16)
    return high, low


def dot3(a, b):
    f = functools.partial(jnp.dot, preferred_element_type=jnp.float32)
    return f(a[0], b[0]) + (f(a[0], b[1]) + f(a[1], b[0]))


def theta_kernel(octants, table_high, table_low, child, out, token, tables, kids, bands, kinds, sems):
    n_kids, n_samp = child.shape[0], out.shape[0]
    loads = [pltpu.make_async_copy(child.at[c], kids.at[c], sems.at[c]) for c in range(n_kids)]
    parts = [
        pltpu.make_async_copy(table, tables.at[i], sems.at[n_kids + i])
        for i, table in enumerate((table_high, table_low))
    ]
    for copy in parts:
        copy.start()
    small = pltpu.make_async_copy(octants, kinds, sems.at[n_kids + 2])
    small.start()
    for copy in loads:
        copy.start()
    small.wait()
    lane = lax.broadcasted_iota(jnp.int32, (8, 128), 1)
    v = jnp.zeros((8, 128), jnp.int32)
    for i in range(8):
        v = jnp.where(lane == i, kinds[0, i], v)
    v = v.astype(jnp.float32)
    for s in range(n_samp):
        bands[s, 384:392, :] = v
    token[...] = v
    stores = []

    def store(first, count):
        rows = pl.ds(first, count)
        stores.append(pltpu.make_async_copy(bands.at[:, rows], out.at[:, rows], sems.at[n_kids + 3 + len(stores)]))
        stores[-1].start()

    for copy in parts:
        copy.wait()
    table = jnp.concatenate([tables[0], tables[0], tables[1]], 1)
    for c in range(n_kids):
        loads[c].wait()
        high, low = split(jnp.concatenate([kids[c, 0], kids[c, 1]], 1))
        y = jnp.dot(table, jnp.concatenate([high, low, high], 0), preferred_element_type=jnp.float32)
        for s in range(n_samp):
            for half in range(2):
                at = 192 * half + 24 * c
                for k in range(2):
                    cols = slice(256 * k + 128 * half, 256 * k + 128 * half + 128)
                    bands[s, at + 8 * k : at + 8 * k + 8, :] = y[8 * s : 8 * s + 8, cols]
                    rest = y[128 + 4 * s : 132 + 4 * s, cols]
                    bands[s, at + 16 + 4 * k : at + 20 + 4 * k, :] = rest
        store(24 * c, 24)
        store(192 + 24 * c, 24 + 8 * (c == n_kids - 1))
    for copy in stores:
        copy.wait()


def prepare_kernel(box, token, table, out, done, raw, sems):
    me = box[0]
    n_off = table.shape[0]
    pair, half = me // 2, me % 2
    copies = []
    for q in range(5):
        at = 4 * me + q if q < 4 else 32 + pair
        lanes = pl.ds(pl.multiple_of(128 * (at % 3), 128), 128)
        copies.append(
            pltpu.make_async_copy(table.at[:, at // 3, :, lanes], raw.at[:, q], sems.at[q])
        )
        copies[-1].start()
    done[...] = token[...]
    for copy in copies:
        copy.wait()
    left = lax.broadcasted_iota(jnp.int32, (1, 128), 1) < 64
    upper = jnp.full((1, 128), half, jnp.int32) == 1

    def one(i, carry):
        out[i, 0:8] = jnp.concatenate([raw[i, q] for q in range(4)], 0)
        re, im = raw[i, 4, 0:1], raw[i, 4, 1:2]
        x = jnp.where(left, re, pltpu.roll(im, 64, 1))
        y = jnp.where(left, pltpu.roll(re, 64, 1), im)
        out[i, 8:16] = jnp.broadcast_to(jnp.where(upper, y, x), (8, 128))
        return carry

    lax.fori_loop(0, n_off // 4, lambda i, c: [one(4 * i + u, c) for u in range(4)][-1], 0)


def phi_kernel(
    owners, token, lists, table_high, table_low, cos_hbm, sin_hbm, recv, send,
    total, fine, rows_v, send_v, tables, cos_ref, sin_ref, kinds_v, kinds, sems,
):
    pairs = [(table_high, tables.at[0]), (table_low, tables.at[1]), (cos_hbm, cos_ref), (sin_hbm, sin_ref)]
    loads = [pltpu.make_async_copy(a, b, sems.at[i]) for i, (a, b) in enumerate(pairs)]
    for copy in loads:
        copy.start()
    for s in range(16):
        kinds_v[s : s + 1, :] = recv[s, 384:385, :].astype(jnp.int32)
    copy = pltpu.make_async_copy(kinds_v, kinds, sems.at[4])
    copy.start()
    total[...] = jnp.zeros_like(total)
    for d in range(8):
        send_v[d, 288:312, :] = lists[...]
    for load in loads[:2]:
        load.wait()
    table = jnp.concatenate([tables[0], tables[0], tables[1]], 0)

    def product(s):
        high, low = split(jnp.concatenate([recv[s, 0:192, :], recv[s, 192:384, :]], 1))
        return jnp.dot(jnp.concatenate([high, low, high], 1), table, preferred_element_type=jnp.float32)

    def add(s, fine):
        for c in range(8):
            child = s * 8 + c
            owner, octant = owners[child], kinds[s, c]
            f = fine[24 * c : 24 * c + 24, :]
            cos_0, sin_0 = cos_ref[octant, 0:8], sin_ref[octant, 0:8]
            total[owner, 0:8] += cos_0 * f[0:8] - sin_0 * f[8:16]
            total[owner, 8:16] += sin_0 * f[0:8] + cos_0 * f[8:16]
            swapped = pltpu.roll(f[16:24], 4, 0)
            total[owner, 16:24] += cos_ref[octant, 8:16] * f[16:24] + sin_ref[octant, 8:16] * swapped

    fine[0] = product(0)
    for load in loads[2:]:
        load.wait()
    copy.wait()

    def two(i, carry):
        s = 2 * i
        fine[1] = product(s + 1)
        add(s, fine.at[0])
        fine[0] = product(lax.rem(s + 2, 16))
        add(s + 1, fine.at[1])
        return carry

    lax.fori_loop(0, 8, two, 0, unroll=2)

    def parent(p, carry):
        for l in range(3):
            v = total[p, :, 128 * l : 128 * l + 128]
            base = 72 * p + 2 * l
            rows_v[pl.ds(base, 8, stride=6), :] = v[0:8]
            rows_v[pl.ds(base + 1, 8, stride=6), :] = v[8:16]
            rows_v[pl.ds(base + 48, 4, stride=6), :] = v[16:20]
            rows_v[pl.ds(base + 49, 4, stride=6), :] = v[20:24]
        for d in range(8):
            at = pl.multiple_of(72 * p + 8 * d, 8)
            send_v[d, pl.ds(pl.multiple_of(8 * p, 8), 8), :] = rows_v[pl.ds(at, 8), :]
        return carry

    left = lax.broadcasted_iota(jnp.int32, (8, 128), 1) < 64
    copies = []
    for q in range(4):
        lax.fori_loop(8 * q, 8 * q + 8, parent, 0)
        rows = pl.ds(64 * q, 64)
        copies.append(pltpu.make_async_copy(send_v.at[:, rows], send.at[:, rows], sems.at[5 + q]))
        copies[-1].start()
        for r in range(4):
            at = 72 * 8 * q + 64 + 2 * r
            re, im = rows_v[pl.ds(at, 8, stride=72), :], rows_v[pl.ds(at + 1, 8, stride=72), :]
            rows = slice(256 + 8 * q, 264 + 8 * q)
            send_v[2 * r, rows, :] = jnp.where(left, re, pltpu.roll(im, 64, 1))
            send_v[2 * r + 1, rows, :] = jnp.where(left, pltpu.roll(re, 64, 1), im)
    rows = pl.ds(256, 56)
    copies.append(pltpu.make_async_copy(send_v.at[:, rows], send.at[:, rows], sems.at[9]))
    copies[-1].start()
    for copy in copies:
        copy.wait()


def translate_kernel(recv, factor, send, source, sums, send_v, idx_v, idx, load_sems, store_sems):
    n_far, n_own = 48, 32
    loads = []
    for b in range(8):
        rows = pl.ds(24 * b, 24)
        idx_v[rows, :] = recv[b, 288:312, :].astype(jnp.int32)
        loads.append(pltpu.make_async_copy(idx_v.at[rows], idx.at[rows], load_sems.at[b]))
        loads[-1].start()
    left = lax.broadcasted_iota(jnp.int32, (8, 128), 1) < 64
    even = lax.broadcasted_iota(jnp.int32, (8, 128), 0) % 2 == 0
    for b in range(8):

        def prepare(p, carry):
            v = recv[b, pl.ds(pl.multiple_of(8 * p, 8), 8), :]
            at = pl.multiple_of((b * n_own + p) * 24, 8)
            source[pl.ds(at, 8), :] = jnp.where(even, v, pltpu.roll(v, 1, 0))
            source[pl.ds(at + 8, 8), :] = jnp.where(even, pltpu.roll(v, 7, 0), v)
            return carry

        lax.fori_loop(0, n_own, prepare, 0, unroll=8)
        for q in range(4):
            v = recv[b, 256 + 8 * q : 264 + 8 * q, :]
            r = pltpu.roll(v, 64, 1)
            at = (b * n_own + 8 * q) * 24 + 16
            source[pl.ds(at, 8, stride=24), :] = jnp.where(left, v, r)
            source[pl.ds(at + 1, 8, stride=24), :] = jnp.where(left, r, v)

    def index(j, b, p):
        return pl.multiple_of(idx.at[pl.ds(j // 4, 169), pl.ds(n_own * (j % 4), n_own)][24 * b, p], 8)

    def some(i, b):
        acc = [[jnp.zeros((8, 128), jnp.float32) for _ in range(3)] for _ in range(8)]
        for j in range(n_far):
            for h in range(8):
                f, o = index(j, b, 8 * i + h), index(n_far + j, b, 8 * i + h)
                t = factor[pl.ds(o, 8), :]
                acc[h][0] += t * source[pl.ds(f, 8), :]
                acc[h][1] += t * source[pl.ds(f + 8, 8), :]
                acc[h][2] += factor[pl.ds(o + 8, 8), :] * source[pl.ds(f + 16, 8), :]
        for h in range(8):
            for k in range(3):
                sums[pl.ds(pl.multiple_of(24 * (b * n_own + 8 * i), 8) + 24 * h + 8 * k, 8), :] = acc[h][k]
        return b

    def finish(p, b):
        at = pl.multiple_of((b * n_own + p) * 24, 8)
        r = sums[pl.ds(at + 8, 8), :]
        r = jnp.where(even, -pltpu.roll(r, 7, 0), pltpu.roll(r, 1, 0))
        send_v[b, pl.ds(pl.multiple_of(8 * p, 8), 8), :] = sums[pl.ds(at, 8), :] + r
        return b

    def store(b):
        return pltpu.make_async_copy(send_v.at[pl.ds(b, 1)], send.at[pl.ds(b, 1)], store_sems.at[b])

    def box(b, carry):
        rows = pl.ds(pl.multiple_of(24 * b, 8), 24)
        pltpu.make_async_copy(idx_v.at[rows], idx.at[rows], load_sems.at[b]).wait()
        lax.fori_loop(0, n_own // 8, some, b)
        lax.fori_loop(0, n_own, finish, b, unroll=8)
        for q in range(4):
            at = (b * n_own + 8 * q) * 24 + 16
            r = pltpu.roll(sums[pl.ds(at + 1, 8, stride=24), :], 64, 1)
            rows = slice(256 + 8 * q, 264 + 8 * q)
            send_v[b, rows, :] = sums[pl.ds(at, 8, stride=24), :] + jnp.where(left, -r, r)
        store(b).start()
        return carry

    lax.fori_loop(0, 8, box, 0)
    for b in range(8):
        store(b).wait()


def place_kernel(recv, out, last, out_v, sems):
    left = lax.broadcasted_iota(jnp.int32, (8, 128), 1) < 64
    copies = []
    for q in range(4):
        for r in range(4):
            rows = slice(256 + 8 * q, 264 + 8 * q)
            e, o = recv[2 * r, rows, :], recv[2 * r + 1, rows, :]
            at = 8 * 8 * q + 2 * r
            last[pl.ds(at, 8, stride=8), :] = jnp.where(left, e, pltpu.roll(o, 64, 1))
            last[pl.ds(at + 1, 8, stride=8), :] = jnp.where(left, pltpu.roll(e, 64, 1), o)

        def one(p, carry):
            base = pl.multiple_of(8 * p, 8)
            for at in range(36):
                rows = pl.ds(base + 2 * (at % 4), 2)
                v = recv[at // 4, rows, :] if at < 32 else last[rows, :]
                out_v[p, at // 3, :, 128 * (at % 3) : 128 * (at % 3) + 128] = v
            return carry

        lax.fori_loop(8 * q, 8 * q + 8, one, 0)
        some = pl.ds(8 * q, 8)
        copies.append(pltpu.make_async_copy(out_v.at[some], out.at[some], sems.at[q]))
        copies[-1].start()
    for copy in copies:
        copy.wait()


def phase_tables(samp, n_theta, n_phi):
    polar = np.concatenate([np.arange(12), np.arange(8, 12)])
    sign = np.where((np.arange(16) >= 8) & (np.arange(16) < 12), -1.0, 1.0).astype(np.float32)
    theta = (samp * 12 + polar).astype(jnp.float32) * (math.pi / n_theta) + 0.5 * math.pi / n_theta
    phi = np.arange(n_phi) * (2.0 * math.pi / n_phi)
    o = np.arange(8)
    sx, sy, sz = 1.0 - 2 * (o % 2), 1.0 - 2 * (o // 2 % 2), 1.0 - 2 * (o // 4)
    around = (sx[:, None] * np.cos(phi) + sy[:, None] * np.sin(phi)).astype(np.float32)
    angle = phase_scale * (
        jnp.sin(theta)[None, :, None] * around[:, None, :]
        + (sz.astype(np.float32)[:, None] * jnp.cos(theta)[None, :])[:, :, None]
    )
    return jnp.cos(angle), jnp.sin(angle) * sign[None, :, None]


def vmem():
    return pl.BlockSpec(memory_space=pltpu.VMEM)


def smem():
    return pl.BlockSpec(memory_space=pltpu.SMEM)


def held(x):
    return pltpu.with_memory_space_constraint(x, pltpu.VMEM)


def params(mib):
    return pltpu.CompilerParams(vmem_limit_bytes=mib * 2**20)


def anywhere():
    return pl.BlockSpec(memory_space=pl.ANY)


def far_away(x):
    return pltpu.with_memory_space_constraint(x, pltpu.HBM)


def shards(child_patterns, octants, parent_map, far_boxes, offsets, translation):
    n_box, n_samp = lax.axis_size("box"), lax.axis_size("samp")
    count, _, n_t1, n_p1 = child_patterns.shape
    n_off, _, band, n_p2 = translation.shape
    n_t2 = band * n_samp
    parents, n_far = far_boxes.shape
    box, samp = lax.axis_index("box"), lax.axis_index("samp")
    f32, bf16 = jnp.float32, jnp.bfloat16

    theta_table = lagrange_table(n_t1, n_t2, False).reshape(n_samp, band, n_t1)
    parts = [theta_table[:, 0:8].reshape(-1, n_t1), theta_table[:, 8:12].reshape(-1, n_t1)]
    theta_high, theta_low = high_low(np.concatenate(parts))
    phi_high, phi_low = high_low(lagrange_table(n_p1, n_p2, True).T)

    sent = (n_samp, 48 * count + 8, 128)
    bands, token = pl.pallas_call(
        theta_kernel,
        in_specs=[anywhere()] * 4,
        out_specs=[anywhere(), vmem()],
        out_shape=[pltpu.HBM(sent, f32), jax.ShapeDtypeStruct((8, 128), f32)],
        scratch_shapes=[
            pltpu.VMEM((2, n_t2, n_t1), bf16),
            pltpu.VMEM(child_patterns.shape, f32),
            pltpu.VMEM(sent, f32),
            pltpu.SMEM((1, count), jnp.int32),
            pltpu.SemaphoreType.DMA((3 * count + 3,)),
        ],
        compiler_params=params(9),
        name="theta",
    )(far_away(octants.reshape(1, count)), far_away(theta_high), far_away(theta_low), far_away(child_patterns))
    bands = lax.all_to_all(bands, "samp", 0, 0)

    cos_part, sin_part = phase_tables(samp, n_t2, n_p2)
    factor, token = pl.pallas_call(
        prepare_kernel,
        in_specs=[smem(), vmem(), anywhere()],
        out_specs=[vmem()] * 2,
        out_shape=[pltpu.VMEM((n_off, 16, 128), f32), jax.ShapeDtypeStruct((8, 128), f32)],
        scratch_shapes=[pltpu.VMEM((n_off, 5, 2, 128), f32), pltpu.SemaphoreType.DMA((5,))],
        compiler_params=params(6),
        cost_estimate=pl.CostEstimate(flops=10**7, bytes_accessed=10**7, transcendentals=0),
        name="prepare",
    )(box.reshape(1), token, far_away(translation.transpose(0, 2, 1, 3)))
    lists = jnp.concatenate([far_boxes.T * 24, offsets.T * 16], 0).reshape(24, 128)

    send = pl.pallas_call(
        phi_kernel,
        in_specs=[smem(), vmem(), vmem()] + [anywhere()] * 4 + [vmem()],
        out_specs=anywhere(),
        out_shape=pltpu.HBM((n_box, 9 * parents + 24, 128), f32),
        scratch_shapes=[
            pltpu.VMEM((parents, 24, n_p2), f32),
            pltpu.VMEM((2, 24 * count, n_p2), f32),
            pltpu.VMEM((parents * 72, 128), f32),
            pltpu.VMEM((n_box, 9 * parents + 24, 128), f32),
            pltpu.VMEM((2, n_p1, n_p2), bf16),
            pltpu.VMEM(cos_part.shape, f32),
            pltpu.VMEM(cos_part.shape, f32),
            pltpu.VMEM((n_samp, 128), jnp.int32),
            pltpu.SMEM((n_samp, 128), jnp.int32),
            pltpu.SemaphoreType.DMA((10,)),
        ],
        compiler_params=params(12),
        name="phi",
    )(
        parent_map[0], token, lists.astype(f32),
        *[far_away(x) for x in (phi_high, phi_low, cos_part, sin_part)], held(bands),
    )

    everywhere = lax.all_to_all(send, "box", 0, 0)
    n_all = n_box * parents
    back = pl.pallas_call(
        translate_kernel,
        in_specs=[vmem(), vmem()],
        out_specs=anywhere(),
        out_shape=pltpu.HBM((n_box, 9 * parents, 128), f32),
        scratch_shapes=[
            pltpu.VMEM((n_all * 24, 128), f32),
            pltpu.VMEM((n_all * 24, 128), f32),
            pltpu.VMEM((n_box, 9 * parents, 128), f32),
            pltpu.VMEM((24 * n_box, 128), jnp.int32),
            pltpu.SMEM((24 * n_box, 128), jnp.int32),
            pltpu.SemaphoreType.DMA((n_box,)),
            pltpu.SemaphoreType.DMA((n_box,)),
        ],
        compiler_params=params(12),
        name="translate",
    )(held(everywhere), held(factor.reshape(n_off * 16, 128)))
    back = lax.all_to_all(back, "box", 0, 0)
    shape = (parents, band, 2, n_p2)
    place = pl.pallas_call(
        place_kernel,
        in_specs=[vmem()],
        out_specs=anywhere(),
        out_shape=pltpu.HBM(shape, f32),
        scratch_shapes=[
            pltpu.VMEM((8 * parents, 128), f32),
            pltpu.VMEM(shape, f32),
            pltpu.SemaphoreType.DMA((4,)),
        ],
        compiler_params=params(6),
        cost_estimate=pl.CostEstimate(flops=10**6, bytes_accessed=4 * 10**6, transcendentals=0),
        name="place",
    )
    outgoing, incoming = place(send), place(held(back))
    return outgoing.transpose(0, 2, 1, 3), incoming.transpose(0, 2, 1, 3)


def solution(mesh):
    in_specs = (
        P(("box", "samp"), None, None, None),
        P(("box", "samp")),
        P("box", None),
        P("box", None),
        P("box", None),
        P(None, None, "samp", None),
    )
    out_specs = (P("box", None, "samp", None), P("box", None, "samp", None))
    return jax.shard_map(shards, mesh=mesh, in_specs=in_specs, out_specs=out_specs, check_vma=False)
```

```python
import functools
import math

import jax
import jax.numpy as jnp
import numpy as np
from jax import lax
from jax.experimental import pallas as pl
from jax.experimental.pallas import tpu as pltpu
from jax.sharding import PartitionSpec as P

phase_scale = 12.0


def lagrange_table(n_old, n_new, periodic):
    rows = np.arange(n_new)
    if periodic:
        numer, denom = rows * n_old, n_new
    else:
        numer, denom = (2 * rows + 1) * n_old - n_new, 2 * n_new
    start = numer // denom - 2
    if not periodic:
        start = np.clip(start, 0, n_old - 6)
    position = numer / denom - start
    table = np.zeros((n_new, n_old))
    for node in range(6):
        weight = np.ones(n_new)
        for other in range(6):
            if other != node:
                weight = weight * (position - other) / (node - other)
        target = start + node
        if periodic:
            target = target % n_old
        table[rows, target] += weight
    return table


def high_low(table):
    table = table.astype(np.float32)
    high = table.astype(jnp.bfloat16)
    low = (table - high.astype(np.float32)).astype(jnp.bfloat16)
    return high, low


def split(x):
    high = x.astype(jnp.bfloat16)
    low = (x - high.astype(jnp.float32)).astype(jnp.bfloat16)
    return high, low


def dot3(a, b):
    f = functools.partial(jnp.dot, preferred_element_type=jnp.float32)
    return f(a[0], b[0]) + (f(a[0], b[1]) + f(a[1], b[0]))


def theta_kernel(octants, table_high, table_low, child, out, token, tables, kids, bands, kinds, sems):
    n_kids, n_samp = child.shape[0], out.shape[0]
    loads = [pltpu.make_async_copy(child.at[c], kids.at[c], sems.at[c]) for c in range(n_kids)]
    parts = [
        pltpu.make_async_copy(table, tables.at[i], sems.at[n_kids + i])
        for i, table in enumerate((table_high, table_low))
    ]
    for copy in parts:
        copy.start()
    small = pltpu.make_async_copy(octants, kinds, sems.at[n_kids + 2])
    small.start()
    for copy in loads:
        copy.start()
    small.wait()
    lane = lax.broadcasted_iota(jnp.int32, (8, 128), 1)
    v = jnp.zeros((8, 128), jnp.int32)
    for i in range(8):
        v = jnp.where(lane == i, kinds[0, i], v)
    v = v.astype(jnp.float32)
    for s in range(n_samp):
        bands[s, 384:392, :] = v
    token[...] = v
    stores = []

    def store(first, count):
        rows = pl.ds(first, count)
        stores.append(pltpu.make_async_copy(bands.at[:, rows], out.at[:, rows], sems.at[n_kids + 3 + len(stores)]))
        stores[-1].start()

    for copy in parts:
        copy.wait()
    table = jnp.concatenate([tables[0], tables[0], tables[1]], 1)
    for c in range(n_kids):
        loads[c].wait()
        high, low = split(jnp.concatenate([kids[c, 0], kids[c, 1]], 1))
        y = jnp.dot(table, jnp.concatenate([high, low, high], 0), preferred_element_type=jnp.float32)
        for s in range(n_samp):
            for half in range(2):
                at = 192 * half + 24 * c
                for k in range(2):
                    cols = slice(256 * k + 128 * half, 256 * k + 128 * half + 128)
                    bands[s, at + 8 * k : at + 8 * k + 8, :] = y[8 * s : 8 * s + 8, cols]
                    rest = y[128 + 4 * s : 132 + 4 * s, cols]
                    bands[s, at + 16 + 4 * k : at + 20 + 4 * k, :] = rest
        store(24 * c, 24)
        store(192 + 24 * c, 24 + 8 * (c == n_kids - 1))
    for copy in stores:
        copy.wait()


def prepare_kernel(box, token, lists, table, out, done, lists_out, raw, sems):
    me = box[0]
    n_off = table.shape[0]
    pair, half = me // 2, me % 2
    copies = []
    for q in range(5):
        at = 4 * me + q if q < 4 else 32 + pair
        lanes = pl.ds(pl.multiple_of(128 * (at % 3), 128), 128)
        copies.append(
            pltpu.make_async_copy(table.at[:, at // 3, :, lanes], raw.at[:, q], sems.at[q])
        )
        copies[-1].start()
    done[...] = token[...]
    lists_out[...] = lists[...]
    for copy in copies:
        copy.wait()
    left = lax.broadcasted_iota(jnp.int32, (1, 128), 1) < 64
    upper = jnp.full((1, 128), half, jnp.int32) == 1

    def one(i, carry):
        out[i, 0:8] = jnp.concatenate([raw[i, q] for q in range(4)], 0)
        re, im = raw[i, 4, 0:1], raw[i, 4, 1:2]
        x = jnp.where(left, re, pltpu.roll(im, 64, 1))
        y = jnp.where(left, pltpu.roll(re, 64, 1), im)
        out[i, 8:16] = jnp.broadcast_to(jnp.where(upper, y, x), (8, 128))
        return carry

    lax.fori_loop(0, n_off // 4, lambda i, c: [one(4 * i + u, c) for u in range(4)][-1], 0)


def phi_kernel(
    owners, token, lists, table_high, table_low, cos_hbm, sin_hbm, recv, send_v,
    total, fine, rows_v,  tables, cos_ref, sin_ref, kinds_v, kinds, sems,
):
    pairs = [(table_high, tables.at[0]), (table_low, tables.at[1]), (cos_hbm, cos_ref), (sin_hbm, sin_ref)]
    loads = [pltpu.make_async_copy(a, b, sems.at[i]) for i, (a, b) in enumerate(pairs)]
    for copy in loads:
        copy.start()
    for s in range(16):
        kinds_v[s : s + 1, :] = recv[s, 384:385, :].astype(jnp.int32)
    copy = pltpu.make_async_copy(kinds_v, kinds, sems.at[4])
    copy.start()
    total[...] = jnp.zeros_like(total)
    for load in loads[:2]:
        load.wait()
    table = jnp.concatenate([tables[0], tables[0], tables[1]], 0)

    def product(s):
        high, low = split(jnp.concatenate([recv[s, 0:192, :], recv[s, 192:384, :]], 1))
        return jnp.dot(jnp.concatenate([high, low, high], 1), table, preferred_element_type=jnp.float32)

    def add(s, fine):
        for c in range(8):
            child = s * 8 + c
            owner, octant = owners[child], kinds[s, c]
            f = fine[24 * c : 24 * c + 24, :]
            cos_0, sin_0 = cos_ref[octant, 0:8], sin_ref[octant, 0:8]
            total[owner, 0:8] += cos_0 * f[0:8] - sin_0 * f[8:16]
            total[owner, 8:16] += sin_0 * f[0:8] + cos_0 * f[8:16]
            swapped = pltpu.roll(f[16:24], 4, 0)
            total[owner, 16:24] += cos_ref[octant, 8:16] * f[16:24] + sin_ref[octant, 8:16] * swapped

    fine[0] = product(0)
    for load in loads[2:]:
        load.wait()
    copy.wait()

    def two(i, carry):
        s = 2 * i
        fine[1] = product(s + 1)
        add(s, fine.at[0])
        fine[0] = product(lax.rem(s + 2, 16))
        add(s + 1, fine.at[1])
        return carry

    lax.fori_loop(0, 8, two, 0, unroll=2)

    def parent(p, carry):
        for l in range(3):
            v = total[p, :, 128 * l : 128 * l + 128]
            base = 72 * p + 2 * l
            rows_v[pl.ds(base, 8, stride=6), :] = v[0:8]
            rows_v[pl.ds(base + 1, 8, stride=6), :] = v[8:16]
            rows_v[pl.ds(base + 48, 4, stride=6), :] = v[16:20]
            rows_v[pl.ds(base + 49, 4, stride=6), :] = v[20:24]
        for d in range(8):
            at = pl.multiple_of(72 * p + 8 * d, 8)
            send_v[d, pl.ds(pl.multiple_of(8 * p, 8), 8), :] = rows_v[pl.ds(at, 8), :]
        return carry

    left = lax.broadcasted_iota(jnp.int32, (8, 128), 1) < 64
    for q in range(4):
        lax.fori_loop(8 * q, 8 * q + 8, parent, 0)
        for r in range(4):
            at = 72 * 8 * q + 64 + 2 * r
            re, im = rows_v[pl.ds(at, 8, stride=72), :], rows_v[pl.ds(at + 1, 8, stride=72), :]
            rows = slice(256 + 8 * q, 264 + 8 * q)
            send_v[2 * r, rows, :] = jnp.where(left, re, pltpu.roll(im, 64, 1))
            send_v[2 * r + 1, rows, :] = jnp.where(left, pltpu.roll(re, 64, 1), im)


def translate_kernel(box_id, lists, recv, factor, send, source, sums, send_v, idx, load_sems, store_sems):
    n_far, n_own = 48, 32
    me = box_id[0]

    def load(b):
        rows = pl.ds(pl.multiple_of(24 * b, 8), 24)
        return pltpu.make_async_copy(lists.at[lax.bitwise_xor(me, b)], idx.at[rows], load_sems.at[b])

    for b in range(8):
        load(jnp.int32(b)).start()
    left = lax.broadcasted_iota(jnp.int32, (8, 128), 1) < 64
    even = lax.broadcasted_iota(jnp.int32, (8, 128), 0) % 2 == 0
    for b in range(8):

        def prepare(p, carry):
            v = recv[b, pl.ds(pl.multiple_of(8 * p, 8), 8), :]
            at = pl.multiple_of((b * n_own + p) * 24, 8)
            source[pl.ds(at, 8), :] = jnp.where(even, v, pltpu.roll(v, 1, 0))
            source[pl.ds(at + 8, 8), :] = jnp.where(even, pltpu.roll(v, 7, 0), v)
            return carry

        lax.fori_loop(0, n_own, prepare, 0, unroll=8)
        for q in range(4):
            v = recv[b, 256 + 8 * q : 264 + 8 * q, :]
            r = pltpu.roll(v, 64, 1)
            at = (b * n_own + 8 * q) * 24 + 16
            source[pl.ds(at, 8, stride=24), :] = jnp.where(left, v, r)
            source[pl.ds(at + 1, 8, stride=24), :] = jnp.where(left, r, v)

    def index(j, b, p):
        return pl.multiple_of(idx.at[pl.ds(j // 4, 169), pl.ds(n_own * (j % 4), n_own)][24 * b, p], 8)

    def some(i, b):
        acc = [[jnp.zeros((8, 128), jnp.float32) for _ in range(3)] for _ in range(8)]
        for j in range(n_far):
            for h in range(8):
                f, o = index(j, b, 8 * i + h), index(n_far + j, b, 8 * i + h)
                t = factor[pl.ds(o, 8), :]
                acc[h][0] += t * source[pl.ds(f, 8), :]
                acc[h][1] += t * source[pl.ds(f + 8, 8), :]
                acc[h][2] += factor[pl.ds(o + 8, 8), :] * source[pl.ds(f + 16, 8), :]
        for h in range(8):
            for k in range(3):
                sums[pl.ds(pl.multiple_of(24 * (b * n_own + 8 * i), 8) + 24 * h + 8 * k, 8), :] = acc[h][k]
        return b

    def finish(p, b):
        at = pl.multiple_of((b * n_own + p) * 24, 8)
        r = sums[pl.ds(at + 8, 8), :]
        r = jnp.where(even, -pltpu.roll(r, 7, 0), pltpu.roll(r, 1, 0))
        send_v[b, pl.ds(pl.multiple_of(8 * p, 8), 8), :] = sums[pl.ds(at, 8), :] + r
        return b

    def store(b):
        return pltpu.make_async_copy(send_v.at[pl.ds(b, 1)], send.at[pl.ds(b, 1)], store_sems.at[b])

    def box(b, carry):
        load(b).wait()
        lax.fori_loop(0, n_own // 8, some, b)
        lax.fori_loop(0, n_own, finish, b, unroll=8)
        for q in range(4):
            at = (b * n_own + 8 * q) * 24 + 16
            r = pltpu.roll(sums[pl.ds(at + 1, 8, stride=24), :], 64, 1)
            rows = slice(256 + 8 * q, 264 + 8 * q)
            send_v[b, rows, :] = sums[pl.ds(at, 8, stride=24), :] + jnp.where(left, -r, r)
        store(b).start()
        return carry

    lax.fori_loop(0, 8, box, 0)
    for b in range(8):
        store(b).wait()


def place_kernel(recv, out, last, out_v, sems):
    left = lax.broadcasted_iota(jnp.int32, (8, 128), 1) < 64
    copies = []
    for q in range(4):
        for r in range(4):
            rows = slice(256 + 8 * q, 264 + 8 * q)
            e, o = recv[2 * r, rows, :], recv[2 * r + 1, rows, :]
            at = 8 * 8 * q + 2 * r
            last[pl.ds(at, 8, stride=8), :] = jnp.where(left, e, pltpu.roll(o, 64, 1))
            last[pl.ds(at + 1, 8, stride=8), :] = jnp.where(left, pltpu.roll(e, 64, 1), o)

        def one(p, carry):
            base = pl.multiple_of(8 * p, 8)
            for at in range(36):
                rows = pl.ds(base + 2 * (at % 4), 2)
                v = recv[at // 4, rows, :] if at < 32 else last[rows, :]
                out_v[p, at // 3, :, 128 * (at % 3) : 128 * (at % 3) + 128] = v
            return carry

        lax.fori_loop(8 * q, 8 * q + 8, one, 0)
        some = pl.ds(8 * q, 8)
        copies.append(pltpu.make_async_copy(out_v.at[some], out.at[some], sems.at[q]))
        copies[-1].start()
    for copy in copies:
        copy.wait()


def phase_tables(samp, n_theta, n_phi):
    polar = np.concatenate([np.arange(12), np.arange(8, 12)])
    sign = np.where((np.arange(16) >= 8) & (np.arange(16) < 12), -1.0, 1.0).astype(np.float32)
    theta = (samp * 12 + polar).astype(jnp.float32) * (math.pi / n_theta) + 0.5 * math.pi / n_theta
    phi = np.arange(n_phi) * (2.0 * math.pi / n_phi)
    o = np.arange(8)
    sx, sy, sz = 1.0 - 2 * (o % 2), 1.0 - 2 * (o // 2 % 2), 1.0 - 2 * (o // 4)
    around = (sx[:, None] * np.cos(phi) + sy[:, None] * np.sin(phi)).astype(np.float32)
    angle = phase_scale * (
        jnp.sin(theta)[None, :, None] * around[:, None, :]
        + (sz.astype(np.float32)[:, None] * jnp.cos(theta)[None, :])[:, :, None]
    )
    return jnp.cos(angle), jnp.sin(angle) * sign[None, :, None]


def vmem():
    return pl.BlockSpec(memory_space=pltpu.VMEM)


def smem():
    return pl.BlockSpec(memory_space=pltpu.SMEM)


def held(x):
    return pltpu.with_memory_space_constraint(x, pltpu.VMEM)


def params(mib):
    return pltpu.CompilerParams(vmem_limit_bytes=mib * 2**20)


def anywhere():
    return pl.BlockSpec(memory_space=pl.ANY)


def far_away(x):
    return pltpu.with_memory_space_constraint(x, pltpu.HBM)


def shards(child_patterns, octants, parent_map, far_boxes, offsets, translation):
    n_box, n_samp = lax.axis_size("box"), lax.axis_size("samp")
    count, _, n_t1, n_p1 = child_patterns.shape
    n_off, _, band, n_p2 = translation.shape
    n_t2 = band * n_samp
    parents, n_far = far_boxes.shape
    box, samp = lax.axis_index("box"), lax.axis_index("samp")
    f32, bf16 = jnp.float32, jnp.bfloat16

    theta_table = lagrange_table(n_t1, n_t2, False).reshape(n_samp, band, n_t1)
    parts = [theta_table[:, 0:8].reshape(-1, n_t1), theta_table[:, 8:12].reshape(-1, n_t1)]
    theta_high, theta_low = high_low(np.concatenate(parts))
    phi_high, phi_low = high_low(lagrange_table(n_p1, n_p2, True).T)

    sent = (n_samp, 48 * count + 8, 128)
    bands, token = pl.pallas_call(
        theta_kernel,
        in_specs=[anywhere()] * 4,
        out_specs=[anywhere(), vmem()],
        out_shape=[pltpu.HBM(sent, f32), jax.ShapeDtypeStruct((8, 128), f32)],
        scratch_shapes=[
            pltpu.VMEM((2, n_t2, n_t1), bf16),
            pltpu.VMEM(child_patterns.shape, f32),
            pltpu.VMEM(sent, f32),
            pltpu.SMEM((1, count), jnp.int32),
            pltpu.SemaphoreType.DMA((3 * count + 3,)),
        ],
        compiler_params=params(9),
        name="theta",
    )(far_away(octants.reshape(1, count)), far_away(theta_high), far_away(theta_low), far_away(child_patterns))
    bands = lax.all_to_all(bands, "samp", 0, 0)

    cos_part, sin_part = phase_tables(samp, n_t2, n_p2)
    lists = jnp.concatenate([far_boxes.T * 24, offsets.T * 16], 0).reshape(24, 128).astype(f32)
    factor, token, lists = pl.pallas_call(
        prepare_kernel,
        in_specs=[smem(), vmem(), vmem(), anywhere()],
        out_specs=[vmem()] * 3,
        out_shape=[
            pltpu.VMEM((n_off, 16, 128), f32),
            jax.ShapeDtypeStruct((8, 128), f32),
            jax.ShapeDtypeStruct((24, 128), f32),
        ],
        scratch_shapes=[pltpu.VMEM((n_off, 5, 2, 128), f32), pltpu.SemaphoreType.DMA((5,))],
        compiler_params=params(6),
        cost_estimate=pl.CostEstimate(flops=10**7, bytes_accessed=10**7, transcendentals=0),
        name="prepare",
    )(box.reshape(1), token, lists, far_away(translation.transpose(0, 2, 1, 3)))
    pairs = [[(i, i ^ k) for i in range(n_box)] for k in range(1, n_box)]
    lists = jnp.stack([lists] + [lax.ppermute(lists, "box", p) for p in pairs]).astype(jnp.int32)

    send = pl.pallas_call(
        phi_kernel,
        in_specs=[smem(), vmem()] + [anywhere()] * 5 + [vmem()],
        out_specs=vmem(),
        out_shape=pltpu.VMEM((n_box, 9 * parents, 128), f32),
        scratch_shapes=[
            pltpu.VMEM((parents, 24, n_p2), f32),
            pltpu.VMEM((2, 24 * count, n_p2), f32),
            pltpu.VMEM((parents * 72, 128), f32),
            pltpu.VMEM((2, n_p1, n_p2), bf16),
            pltpu.VMEM(cos_part.shape, f32),
            pltpu.VMEM(cos_part.shape, f32),
            pltpu.VMEM((n_samp, 128), jnp.int32),
            pltpu.SMEM((n_samp, 128), jnp.int32),
            pltpu.SemaphoreType.DMA((10,)),
        ],
        compiler_params=params(12),
        name="phi",
    )(
        parent_map[0], token, far_away(lists),
        *[far_away(x) for x in (phi_high, phi_low, cos_part, sin_part)], held(bands),
    )

    everywhere = lax.all_to_all(send, "box", 0, 0)
    n_all = n_box * parents
    back = pl.pallas_call(
        translate_kernel,
        in_specs=[smem(), anywhere(), vmem(), vmem()],
        out_specs=anywhere(),
        out_shape=pltpu.HBM((n_box, 9 * parents, 128), f32),
        scratch_shapes=[
            pltpu.VMEM((n_all * 24, 128), f32),
            pltpu.VMEM((n_all * 24, 128), f32),
            pltpu.VMEM((n_box, 9 * parents, 128), f32),
            pltpu.SMEM((24 * n_box, 128), jnp.int32),
            pltpu.SemaphoreType.DMA((n_box,)),
            pltpu.SemaphoreType.DMA((n_box,)),
        ],
        compiler_params=params(12),
        name="translate",
    )(box.reshape(1), far_away(lists), held(everywhere), held(factor.reshape(n_off * 16, 128)))
    back = lax.all_to_all(back, "box", 0, 0)
    shape = (parents, band, 2, n_p2)
    place = pl.pallas_call(
        place_kernel,
        in_specs=[vmem()],
        out_specs=anywhere(),
        out_shape=pltpu.HBM(shape, f32),
        scratch_shapes=[
            pltpu.VMEM((8 * parents, 128), f32),
            pltpu.VMEM(shape, f32),
            pltpu.SemaphoreType.DMA((4,)),
        ],
        compiler_params=params(6),
        cost_estimate=pl.CostEstimate(flops=10**6, bytes_accessed=4 * 10**6, transcendentals=0),
        name="place",
    )
    outgoing, incoming = place(send), place(held(back))
    return outgoing.transpose(0, 2, 1, 3), incoming.transpose(0, 2, 1, 3)


def solution(mesh):
    in_specs = (
        P(("box", "samp"), None, None, None),
        P(("box", "samp")),
        P("box", None),
        P("box", None),
        P("box", None),
        P(None, None, "samp", None),
    )
    out_specs = (P("box", None, "samp", None), P("box", None, "samp", None))
    return jax.shard_map(shards, mesh=mesh, in_specs=in_specs, out_specs=out_specs, check_vma=False)
```

```python
import functools
import math

import jax
import jax.numpy as jnp
import numpy as np
from jax import lax
from jax.experimental import pallas as pl
from jax.experimental.pallas import tpu as pltpu
from jax.sharding import PartitionSpec as P

phase_scale = 12.0


def lagrange_table(n_old, n_new, periodic):
    rows = np.arange(n_new)
    if periodic:
        numer, denom = rows * n_old, n_new
    else:
        numer, denom = (2 * rows + 1) * n_old - n_new, 2 * n_new
    start = numer // denom - 2
    if not periodic:
        start = np.clip(start, 0, n_old - 6)
    position = numer / denom - start
    table = np.zeros((n_new, n_old))
    for node in range(6):
        weight = np.ones(n_new)
        for other in range(6):
            if other != node:
                weight = weight * (position - other) / (node - other)
        target = start + node
        if periodic:
            target = target % n_old
        table[rows, target] += weight
    return table


def high_low(table):
    table = table.astype(np.float32)
    high = table.astype(jnp.bfloat16)
    low = (table - high.astype(np.float32)).astype(jnp.bfloat16)
    return high, low


def split(x):
    high = x.astype(jnp.bfloat16)
    low = (x - high.astype(jnp.float32)).astype(jnp.bfloat16)
    return high, low


def dot3(a, b):
    f = functools.partial(jnp.dot, preferred_element_type=jnp.float32)
    return f(a[0], b[0]) + (f(a[0], b[1]) + f(a[1], b[0]))


def theta_kernel(octants, table_high, table_low, child, out, token, tables, kids, bands, kinds, sems):
    n_kids, n_samp = child.shape[0], out.shape[0]
    loads = [pltpu.make_async_copy(child.at[c], kids.at[c], sems.at[c]) for c in range(n_kids)]
    parts = [
        pltpu.make_async_copy(table, tables.at[i], sems.at[n_kids + i])
        for i, table in enumerate((table_high, table_low))
    ]
    for copy in parts:
        copy.start()
    small = pltpu.make_async_copy(octants, kinds, sems.at[n_kids + 2])
    small.start()
    for copy in loads:
        copy.start()
    small.wait()
    lane = lax.broadcasted_iota(jnp.int32, (8, 128), 1)
    v = jnp.zeros((8, 128), jnp.int32)
    for i in range(8):
        v = jnp.where(lane == i, kinds[0, i], v)
    v = v.astype(jnp.float32)
    for s in range(n_samp):
        bands[s, 384:392, :] = v
    token[...] = v
    stores = []

    def store(first, count):
        rows = pl.ds(first, count)
        stores.append(pltpu.make_async_copy(bands.at[:, rows], out.at[:, rows], sems.at[n_kids + 3 + len(stores)]))
        stores[-1].start()

    for copy in parts:
        copy.wait()
    table = jnp.concatenate([tables[0], tables[0], tables[1]], 1)
    for c in range(n_kids):
        loads[c].wait()
        high, low = split(jnp.concatenate([kids[c, 0], kids[c, 1]], 1))
        y = jnp.dot(table, jnp.concatenate([high, low, high], 0), preferred_element_type=jnp.float32)
        for s in range(n_samp):
            for half in range(2):
                at = 192 * half + 24 * c
                for k in range(2):
                    cols = slice(256 * k + 128 * half, 256 * k + 128 * half + 128)
                    bands[s, at + 8 * k : at + 8 * k + 8, :] = y[8 * s : 8 * s + 8, cols]
                    rest = y[128 + 4 * s : 132 + 4 * s, cols]
                    bands[s, at + 16 + 4 * k : at + 20 + 4 * k, :] = rest
        store(24 * c, 24)
        store(192 + 24 * c, 24 + 8 * (c == n_kids - 1))
    for copy in stores:
        copy.wait()


def prepare_kernel(box, token, lists, stencil, table, out, stencil_out, lists_out, raw, sems):
    me = box[0]
    n_off = table.shape[0]
    pair, half = me // 2, me % 2
    copies = []
    for q in range(5):
        at = 4 * me + q if q < 4 else 32 + pair
        lanes = pl.ds(pl.multiple_of(128 * (at % 3), 128), 128)
        copies.append(
            pltpu.make_async_copy(table.at[:, at // 3, :, lanes], raw.at[:, q], sems.at[q])
        )
        copies[-1].start()
    stencil_out[...] = stencil[...]
    lists_out[...] = lists[...]
    for copy in copies:
        copy.wait()
    left = lax.broadcasted_iota(jnp.int32, (1, 128), 1) < 64
    upper = jnp.full((1, 128), half, jnp.int32) == 1

    def one(i, carry):
        out[i, 0:8] = jnp.concatenate([raw[i, q] for q in range(4)], 0)
        re, im = raw[i, 4, 0:1], raw[i, 4, 1:2]
        x = jnp.where(left, re, pltpu.roll(im, 64, 1))
        y = jnp.where(left, pltpu.roll(re, 64, 1), im)
        out[i, 8:16] = jnp.broadcast_to(jnp.where(upper, y, x), (8, 128))
        return carry

    lax.fori_loop(0, n_off // 4, lambda i, c: [one(4 * i + u, c) for u in range(4)][-1], 0)


def phi_kernel(
    owners, stencil, lists, cos_hbm, sin_hbm, recv, send_v, total, fine, rows_v, cos_ref, sin_ref, kinds_v, kinds, sems
):
    loads = [pltpu.make_async_copy(a, b, sems.at[i]) for i, (a, b) in enumerate(((cos_hbm, cos_ref), (sin_hbm, sin_ref)))]
    for load in loads:
        load.start()
    for s in range(16):
        kinds_v[s : s + 1, :] = recv[s, 384:385, :].astype(jnp.int32)
    copy = pltpu.make_async_copy(kinds_v, kinds, sems.at[4])
    copy.start()
    total[...] = jnp.zeros_like(total)
    shape = (recv.shape[2] * 2, stencil.shape[1])
    node = (lax.broadcasted_iota(jnp.int32, shape, 0) - stencil[6:7, :].astype(jnp.int32)) & (shape[0] - 1)
    table = jnp.zeros(shape, jnp.float32)
    for i in range(6):
        table = jnp.where(node == i, stencil[i : i + 1, :], table)
    high, low = split(table)
    table = jnp.concatenate([high, high, low], 0)

    def product(s):
        high, low = split(jnp.concatenate([recv[s, 0:192, :], recv[s, 192:384, :]], 1))
        return jnp.dot(jnp.concatenate([high, low, high], 1), table, preferred_element_type=jnp.float32)

    def add(s, fine):
        for c in range(8):
            child = s * 8 + c
            owner, octant = owners[child], kinds[s, c]
            f = fine[24 * c : 24 * c + 24, :]
            cos_0, sin_0 = cos_ref[octant, 0:8], sin_ref[octant, 0:8]
            total[owner, 0:8] += cos_0 * f[0:8] - sin_0 * f[8:16]
            total[owner, 8:16] += sin_0 * f[0:8] + cos_0 * f[8:16]
            swapped = pltpu.roll(f[16:24], 4, 0)
            total[owner, 16:24] += cos_ref[octant, 8:16] * f[16:24] + sin_ref[octant, 8:16] * swapped

    fine[0] = product(0)
    for load in loads:
        load.wait()
    copy.wait()

    def two(i, carry):
        s = 2 * i
        fine[1] = product(s + 1)
        add(s, fine.at[0])
        fine[0] = product(lax.rem(s + 2, 16))
        add(s + 1, fine.at[1])
        return carry

    lax.fori_loop(0, 8, two, 0, unroll=4)

    def parent(p, carry):
        for l in range(3):
            v = total[p, :, 128 * l : 128 * l + 128]
            base = 72 * p + 2 * l
            rows_v[pl.ds(base, 8, stride=6), :] = v[0:8]
            rows_v[pl.ds(base + 1, 8, stride=6), :] = v[8:16]
            rows_v[pl.ds(base + 48, 4, stride=6), :] = v[16:20]
            rows_v[pl.ds(base + 49, 4, stride=6), :] = v[20:24]
        for d in range(8):
            at = pl.multiple_of(72 * p + 8 * d, 8)
            send_v[d, pl.ds(pl.multiple_of(8 * p, 8), 8), :] = rows_v[pl.ds(at, 8), :]
        return carry

    left = lax.broadcasted_iota(jnp.int32, (8, 128), 1) < 64
    for q in range(4):
        lax.fori_loop(8 * q, 8 * q + 8, parent, 0, unroll=4)
        for r in range(4):
            at = 72 * 8 * q + 64 + 2 * r
            re, im = rows_v[pl.ds(at, 8, stride=72), :], rows_v[pl.ds(at + 1, 8, stride=72), :]
            rows = slice(256 + 8 * q, 264 + 8 * q)
            send_v[2 * r, rows, :] = jnp.where(left, re, pltpu.roll(im, 64, 1))
            send_v[2 * r + 1, rows, :] = jnp.where(left, pltpu.roll(re, 64, 1), im)


def translate_kernel(box_id, lists, recv, factor, send, source, sums, send_v, idx, load_sems, store_sems):
    n_far, n_own = 48, 32
    me = box_id[0]

    def load(b):
        rows = pl.ds(pl.multiple_of(24 * b, 8), 24)
        away = lax.bitwise_xor(me, b)
        return pltpu.make_async_copy(lists.at[2 * (away & 3) + (away >> 2)], idx.at[rows], load_sems.at[b])

    for b in range(8):
        load(jnp.int32(b)).start()
    left = lax.broadcasted_iota(jnp.int32, (8, 128), 1) < 64
    even = lax.broadcasted_iota(jnp.int32, (8, 128), 0) % 2 == 0
    for b in range(8):

        def prepare(p, carry):
            v = recv[b, pl.ds(pl.multiple_of(8 * p, 8), 8), :]
            at = pl.multiple_of((b * n_own + p) * 24, 8)
            source[pl.ds(at, 8), :] = jnp.where(even, v, pltpu.roll(v, 1, 0))
            source[pl.ds(at + 8, 8), :] = jnp.where(even, pltpu.roll(v, 7, 0), v)
            return carry

        lax.fori_loop(0, n_own, prepare, 0, unroll=8)
        for q in range(4):
            v = recv[b, 256 + 8 * q : 264 + 8 * q, :]
            r = pltpu.roll(v, 64, 1)
            at = (b * n_own + 8 * q) * 24 + 16
            source[pl.ds(at, 8, stride=24), :] = jnp.where(left, v, r)
            source[pl.ds(at + 1, 8, stride=24), :] = jnp.where(left, r, v)

    def index(j, b, p):
        return pl.multiple_of(idx.at[pl.ds(j // 4, 169), pl.ds(n_own * (j % 4), n_own)][24 * b, p], 8)

    def some(i, b):
        acc = [[jnp.zeros((8, 128), jnp.float32) for _ in range(3)] for _ in range(8)]
        for j in range(n_far):
            for h in range(8):
                f, o = index(j, b, 8 * i + h), index(n_far + j, b, 8 * i + h)
                t = factor[pl.ds(o, 8), :]
                acc[h][0] += t * source[pl.ds(f, 8), :]
                acc[h][1] += t * source[pl.ds(f + 8, 8), :]
                acc[h][2] += factor[pl.ds(o + 8, 8), :] * source[pl.ds(f + 16, 8), :]
        for h in range(8):
            for k in range(3):
                sums[pl.ds(pl.multiple_of(24 * (b * n_own + 8 * i), 8) + 24 * h + 8 * k, 8), :] = acc[h][k]
        return b

    def finish(p, b):
        at = pl.multiple_of((b * n_own + p) * 24, 8)
        r = sums[pl.ds(at + 8, 8), :]
        r = jnp.where(even, -pltpu.roll(r, 7, 0), pltpu.roll(r, 1, 0))
        send_v[b, pl.ds(pl.multiple_of(8 * p, 8), 8), :] = sums[pl.ds(at, 8), :] + r
        return b

    def store(b):
        return pltpu.make_async_copy(send_v.at[pl.ds(b, 1)], send.at[pl.ds(b, 1)], store_sems.at[b])

    def box(b, carry):
        load(b).wait()
        lax.fori_loop(0, n_own // 8, some, b)
        lax.fori_loop(0, n_own, finish, b, unroll=8)
        for q in range(4):
            at = (b * n_own + 8 * q) * 24 + 16
            r = pltpu.roll(sums[pl.ds(at + 1, 8, stride=24), :], 64, 1)
            rows = slice(256 + 8 * q, 264 + 8 * q)
            send_v[b, rows, :] = sums[pl.ds(at, 8, stride=24), :] + jnp.where(left, -r, r)
        store(b).start()
        return carry

    lax.fori_loop(0, 8, box, 0)
    for b in range(8):
        store(b).wait()


def place_kernel(recv, out, last, out_v, sems):
    left = lax.broadcasted_iota(jnp.int32, (8, 128), 1) < 64
    copies = []
    for q in range(4):
        for r in range(4):
            rows = slice(256 + 8 * q, 264 + 8 * q)
            e, o = recv[2 * r, rows, :], recv[2 * r + 1, rows, :]
            at = 8 * 8 * q + 2 * r
            last[pl.ds(at, 8, stride=8), :] = jnp.where(left, e, pltpu.roll(o, 64, 1))
            last[pl.ds(at + 1, 8, stride=8), :] = jnp.where(left, pltpu.roll(e, 64, 1), o)

        def one(p, carry):
            base = pl.multiple_of(8 * p, 8)
            for at in range(36):
                rows = pl.ds(base + 2 * (at % 4), 2)
                v = recv[at // 4, rows, :] if at < 32 else last[rows, :]
                out_v[p, at // 3, :, 128 * (at % 3) : 128 * (at % 3) + 128] = v
            return carry

        lax.fori_loop(8 * q, 8 * q + 8, one, 0)
        some = pl.ds(8 * q, 8)
        copies.append(pltpu.make_async_copy(out_v.at[some], out.at[some], sems.at[q]))
        copies[-1].start()
    for copy in copies:
        copy.wait()


def phase_tables(samp, n_theta, n_phi):
    polar = np.concatenate([np.arange(12), np.arange(8, 12)])
    sign = np.where((np.arange(16) >= 8) & (np.arange(16) < 12), -1.0, 1.0).astype(np.float32)
    theta = (samp * 12 + polar).astype(jnp.float32) * (math.pi / n_theta) + 0.5 * math.pi / n_theta
    phi = np.arange(n_phi) * (2.0 * math.pi / n_phi)
    o = np.arange(8)
    sx, sy, sz = 1.0 - 2 * (o % 2), 1.0 - 2 * (o // 2 % 2), 1.0 - 2 * (o // 4)
    around = (sx[:, None] * np.cos(phi) + sy[:, None] * np.sin(phi)).astype(np.float32)
    angle = phase_scale * (
        jnp.sin(theta)[None, :, None] * around[:, None, :]
        + (sz.astype(np.float32)[:, None] * jnp.cos(theta)[None, :])[:, :, None]
    )
    return jnp.cos(angle), jnp.sin(angle) * sign[None, :, None]


def vmem():
    return pl.BlockSpec(memory_space=pltpu.VMEM)


def smem():
    return pl.BlockSpec(memory_space=pltpu.SMEM)


def held(x):
    return pltpu.with_memory_space_constraint(x, pltpu.VMEM)


def params(mib):
    return pltpu.CompilerParams(vmem_limit_bytes=mib * 2**20)


def anywhere():
    return pl.BlockSpec(memory_space=pl.ANY)


def far_away(x):
    return pltpu.with_memory_space_constraint(x, pltpu.HBM)


def shards(child_patterns, octants, parent_map, far_boxes, offsets, translation):
    n_box, n_samp = lax.axis_size("box"), lax.axis_size("samp")
    count, _, n_t1, n_p1 = child_patterns.shape
    n_off, _, band, n_p2 = translation.shape
    n_t2 = band * n_samp
    parents, n_far = far_boxes.shape
    box, samp = lax.axis_index("box"), lax.axis_index("samp")
    f32, bf16 = jnp.float32, jnp.bfloat16

    theta_table = lagrange_table(n_t1, n_t2, False).reshape(n_samp, band, n_t1)
    parts = [theta_table[:, 0:8].reshape(-1, n_t1), theta_table[:, 8:12].reshape(-1, n_t1)]
    theta_high, theta_low = high_low(np.concatenate(parts))
    phi_table = lagrange_table(n_p1, n_p2, True)
    first = np.arange(n_p2) * n_p1 // n_p2 - 2
    stencil = np.zeros((8, n_p2), np.float32)
    for i in range(6):
        stencil[i] = phi_table[np.arange(n_p2), (first + i) % n_p1]
    stencil[6] = first % n_p1

    sent = (n_samp, 48 * count + 8, 128)
    bands, token = pl.pallas_call(
        theta_kernel,
        in_specs=[anywhere()] * 4,
        out_specs=[anywhere(), vmem()],
        out_shape=[pltpu.HBM(sent, f32), jax.ShapeDtypeStruct((8, 128), f32)],
        scratch_shapes=[
            pltpu.VMEM((2, n_t2, n_t1), bf16),
            pltpu.VMEM(child_patterns.shape, f32),
            pltpu.VMEM(sent, f32),
            pltpu.SMEM((1, count), jnp.int32),
            pltpu.SemaphoreType.DMA((3 * count + 3,)),
        ],
        compiler_params=params(9),
        name="theta",
    )(far_away(octants.reshape(1, count)), far_away(theta_high), far_away(theta_low), far_away(child_patterns))
    bands = lax.all_to_all(bands, "samp", 0, 0)

    cos_part, sin_part = phase_tables(samp, n_t2, n_p2)
    lists = jnp.concatenate([far_boxes.T * 24, offsets.T * 16], 0).reshape(24, 128).astype(f32)
    factor, stencil, lists = pl.pallas_call(
        prepare_kernel,
        in_specs=[smem(), vmem(), vmem(), vmem(), anywhere()],
        out_specs=[vmem()] * 3,
        out_shape=[
            pltpu.VMEM((n_off, 16, 128), f32),
            jax.ShapeDtypeStruct(stencil.shape, f32),
            jax.ShapeDtypeStruct((24, 128), f32),
        ],
        scratch_shapes=[pltpu.VMEM((n_off, 5, 2, 128), f32), pltpu.SemaphoreType.DMA((5,))],
        compiler_params=params(6),
        cost_estimate=pl.CostEstimate(flops=10**7, bytes_accessed=10**7, transcendentals=0),
        name="prepare",
    )(box.reshape(1), token, lists, stencil, far_away(translation.transpose(0, 2, 1, 3)))
    pairs = [[(i, i ^ k) for i in range(n_box)] for k in range(n_box)]
    lists = jnp.stack([lists, lax.ppermute(lists, "box", pairs[4])])
    lists = jnp.concatenate([lists] + [lax.ppermute(lists, "box", pairs[k]) for k in (1, 2, 3)]).astype(jnp.int32)

    send = pl.pallas_call(
        phi_kernel,
        in_specs=[smem(), vmem()] + [anywhere()] * 3 + [vmem()],
        out_specs=vmem(),
        out_shape=pltpu.VMEM((n_box, 9 * parents, 128), f32),
        scratch_shapes=[
            pltpu.VMEM((parents, 24, n_p2), f32),
            pltpu.VMEM((2, 24 * count, n_p2), f32),
            pltpu.VMEM((parents * 72, 128), f32),
            pltpu.VMEM(cos_part.shape, f32),
            pltpu.VMEM(cos_part.shape, f32),
            pltpu.VMEM((n_samp, 128), jnp.int32),
            pltpu.SMEM((n_samp, 128), jnp.int32),
            pltpu.SemaphoreType.DMA((10,)),
        ],
        compiler_params=params(12),
        name="phi",
    )(
        parent_map[0], stencil, far_away(lists), far_away(cos_part), far_away(sin_part), held(bands),
    )

    everywhere = lax.all_to_all(send, "box", 0, 0)
    n_all = n_box * parents
    back = pl.pallas_call(
        translate_kernel,
        in_specs=[smem(), anywhere(), vmem(), vmem()],
        out_specs=anywhere(),
        out_shape=pltpu.HBM((n_box, 9 * parents, 128), f32),
        scratch_shapes=[
            pltpu.VMEM((n_all * 24, 128), f32),
            pltpu.VMEM((n_all * 24, 128), f32),
            pltpu.VMEM((n_box, 9 * parents, 128), f32),
            pltpu.SMEM((24 * n_box, 128), jnp.int32),
            pltpu.SemaphoreType.DMA((n_box,)),
            pltpu.SemaphoreType.DMA((n_box,)),
        ],
        compiler_params=params(12),
        name="translate",
    )(box.reshape(1), far_away(lists), held(everywhere), held(factor.reshape(n_off * 16, 128)))
    back = lax.all_to_all(back, "box", 0, 0)
    shape = (parents, band, 2, n_p2)
    place = pl.pallas_call(
        place_kernel,
        in_specs=[vmem()],
        out_specs=anywhere(),
        out_shape=pltpu.HBM(shape, f32),
        scratch_shapes=[
            pltpu.VMEM((8 * parents, 128), f32),
            pltpu.VMEM(shape, f32),
            pltpu.SemaphoreType.DMA((4,)),
        ],
        compiler_params=params(6),
        cost_estimate=pl.CostEstimate(flops=10**6, bytes_accessed=4 * 10**6, transcendentals=0),
        name="place",
    )
    outgoing, incoming = place(send), place(held(back))
    return outgoing.transpose(0, 2, 1, 3), incoming.transpose(0, 2, 1, 3)


def solution(mesh):
    in_specs = (
        P(("box", "samp"), None, None, None),
        P(("box", "samp")),
        P("box", None),
        P("box", None),
        P("box", None),
        P(None, None, "samp", None),
    )
    out_specs = (P("box", None, "samp", None), P("box", None, "samp", None))
    return jax.shard_map(shards, mesh=mesh, in_specs=in_specs, out_specs=out_specs, check_vma=False)
```

```python
import functools
import math

import jax
import jax.numpy as jnp
import numpy as np
from jax import lax
from jax.experimental import pallas as pl
from jax.experimental.pallas import tpu as pltpu
from jax.sharding import PartitionSpec as P

phase_scale = 12.0


def lagrange_table(n_old, n_new, periodic):
    rows = np.arange(n_new)
    if periodic:
        numer, denom = rows * n_old, n_new
    else:
        numer, denom = (2 * rows + 1) * n_old - n_new, 2 * n_new
    start = numer // denom - 2
    if not periodic:
        start = np.clip(start, 0, n_old - 6)
    position = numer / denom - start
    table = np.zeros((n_new, n_old))
    for node in range(6):
        weight = np.ones(n_new)
        for other in range(6):
            if other != node:
                weight = weight * (position - other) / (node - other)
        target = start + node
        if periodic:
            target = target % n_old
        table[rows, target] += weight
    return table


def high_low(table):
    table = table.astype(np.float32)
    high = table.astype(jnp.bfloat16)
    low = (table - high.astype(np.float32)).astype(jnp.bfloat16)
    return high, low


def split(x):
    high = x.astype(jnp.bfloat16)
    low = (x - high.astype(jnp.float32)).astype(jnp.bfloat16)
    return high, low


def dot3(a, b):
    f = functools.partial(jnp.dot, preferred_element_type=jnp.float32)
    return f(a[0], b[0]) + (f(a[0], b[1]) + f(a[1], b[0]))


def theta_kernel(octants, table_high, table_low, child, out, token, tables, kids, bands, kinds, sems):
    n_kids, n_samp = child.shape[0], out.shape[0]
    loads = [pltpu.make_async_copy(child.at[c], kids.at[c], sems.at[c]) for c in range(n_kids)]
    parts = [
        pltpu.make_async_copy(table, tables.at[i], sems.at[n_kids + i])
        for i, table in enumerate((table_high, table_low))
    ]
    for copy in parts:
        copy.start()
    small = pltpu.make_async_copy(octants, kinds, sems.at[n_kids + 2])
    small.start()
    for copy in loads:
        copy.start()
    small.wait()
    lane = lax.broadcasted_iota(jnp.int32, (8, 128), 1)
    v = jnp.zeros((8, 128), jnp.int32)
    for i in range(8):
        v = jnp.where(lane == i, kinds[0, i], v)
    v = v.astype(jnp.float32)
    for s in range(n_samp):
        bands[s, 384:392, :] = v
    token[...] = v
    stores = []

    def store(first, count):
        rows = pl.ds(first, count)
        stores.append(pltpu.make_async_copy(bands.at[:, rows], out.at[:, rows], sems.at[n_kids + 3 + len(stores)]))
        stores[-1].start()

    for copy in parts:
        copy.wait()
    table = jnp.concatenate([tables[0], tables[0], tables[1]], 1)
    for c in range(n_kids):
        loads[c].wait()
        high, low = split(jnp.concatenate([kids[c, 0], kids[c, 1]], 1))
        y = jnp.dot(table, jnp.concatenate([high, low, high], 0), preferred_element_type=jnp.float32)
        for s in range(n_samp):
            for half in range(2):
                at = 192 * half + 24 * c
                for k in range(2):
                    cols = slice(256 * k + 128 * half, 256 * k + 128 * half + 128)
                    bands[s, at + 8 * k : at + 8 * k + 8, :] = y[8 * s : 8 * s + 8, cols]
                    rest = y[128 + 4 * s : 132 + 4 * s, cols]
                    bands[s, at + 16 + 4 * k : at + 20 + 4 * k, :] = rest
        store(24 * c, 24)
        store(192 + 24 * c, 24 + 8 * (c == n_kids - 1))
    for copy in stores:
        copy.wait()


def prepare_kernel(box, token, lists, stencil, table, out, stencil_out, lists_out, raw, sems):
    me = box[0]
    n_off = table.shape[0]
    pair, half = me // 2, me % 2
    copies = []
    for q in range(5):
        at = 4 * me + q if q < 4 else 32 + pair
        lanes = pl.ds(pl.multiple_of(128 * (at % 3), 128), 128)
        copies.append(
            pltpu.make_async_copy(table.at[:, at // 3, :, lanes], raw.at[:, q], sems.at[q])
        )
        copies[-1].start()
    stencil_out[...] = stencil[...]
    lists_out[...] = lists[...]
    for copy in copies:
        copy.wait()
    left = lax.broadcasted_iota(jnp.int32, (1, 128), 1) < 64
    upper = jnp.full((1, 128), half, jnp.int32) == 1

    def one(i, carry):
        out[i, 0:8] = jnp.concatenate([raw[i, q] for q in range(4)], 0)
        re, im = raw[i, 4, 0:1], raw[i, 4, 1:2]
        x = jnp.where(left, re, pltpu.roll(im, 64, 1))
        y = jnp.where(left, pltpu.roll(re, 64, 1), im)
        out[i, 8:16] = jnp.broadcast_to(jnp.where(upper, y, x), (8, 128))
        return carry

    lax.fori_loop(0, n_off // 4, lambda i, c: [one(4 * i + u, c) for u in range(4)][-1], 0)


def phi_kernel(
    owners, stencil, lists, cos_hbm, sin_hbm, recv, send_v, total, fine, rows_v, cos_ref, sin_ref, kinds_v, kinds, sems
):
    loads = [pltpu.make_async_copy(a, b, sems.at[i]) for i, (a, b) in enumerate(((cos_hbm, cos_ref), (sin_hbm, sin_ref)))]
    for load in loads:
        load.start()
    for s in range(16):
        kinds_v[s : s + 1, :] = recv[s, 384:385, :].astype(jnp.int32)
    copy = pltpu.make_async_copy(kinds_v, kinds, sems.at[4])
    copy.start()
    total[...] = jnp.zeros_like(total)
    shape = (recv.shape[2] * 2, stencil.shape[1])
    node = (lax.broadcasted_iota(jnp.int32, shape, 0) - stencil[6:7, :].astype(jnp.int32)) & (shape[0] - 1)
    table = jnp.zeros(shape, jnp.float32)
    for i in range(6):
        table = jnp.where(node == i, stencil[i : i + 1, :], table)
    high, low = split(table)
    table = jnp.concatenate([high, high, low], 0)

    def product(s):
        high, low = split(jnp.concatenate([recv[s, 0:192, :], recv[s, 192:384, :]], 1))
        return jnp.dot(jnp.concatenate([high, low, high], 1), table, preferred_element_type=jnp.float32)

    def add(s, fine):
        for c in range(8):
            child = s * 8 + c
            owner, octant = owners[child], kinds[s, c]
            f = fine[24 * c : 24 * c + 24, :]
            cos_0, sin_0 = cos_ref[octant, 0:8], sin_ref[octant, 0:8]
            total[owner, 0:8] += cos_0 * f[0:8] - sin_0 * f[8:16]
            total[owner, 8:16] += sin_0 * f[0:8] + cos_0 * f[8:16]
            swapped = pltpu.roll(f[16:24], 4, 0)
            total[owner, 16:24] += cos_ref[octant, 8:16] * f[16:24] + sin_ref[octant, 8:16] * swapped

    fine[0] = product(0)
    for load in loads:
        load.wait()
    copy.wait()

    def two(i, carry):
        s = 2 * i
        fine[1] = product(s + 1)
        add(s, fine.at[0])
        fine[0] = product(lax.rem(s + 2, 16))
        add(s + 1, fine.at[1])
        return carry

    lax.fori_loop(0, 8, two, 0, unroll=4)

    def parent(p, carry):
        for l in range(3):
            v = total[p, :, 128 * l : 128 * l + 128]
            base = 72 * p + 2 * l
            rows_v[pl.ds(base, 8, stride=6), :] = v[0:8]
            rows_v[pl.ds(base + 1, 8, stride=6), :] = v[8:16]
            rows_v[pl.ds(base + 48, 4, stride=6), :] = v[16:20]
            rows_v[pl.ds(base + 49, 4, stride=6), :] = v[20:24]
        for d in range(8):
            at = pl.multiple_of(72 * p + 8 * d, 8)
            send_v[d, pl.ds(pl.multiple_of(8 * p, 8), 8), :] = rows_v[pl.ds(at, 8), :]
        return carry

    left = lax.broadcasted_iota(jnp.int32, (8, 128), 1) < 64
    for q in range(4):
        lax.fori_loop(8 * q, 8 * q + 8, parent, 0, unroll=4)
        for r in range(4):
            at = 72 * 8 * q + 64 + 2 * r
            re, im = rows_v[pl.ds(at, 8, stride=72), :], rows_v[pl.ds(at + 1, 8, stride=72), :]
            rows = slice(256 + 8 * q, 264 + 8 * q)
            send_v[2 * r, rows, :] = jnp.where(left, re, pltpu.roll(im, 64, 1))
            send_v[2 * r + 1, rows, :] = jnp.where(left, pltpu.roll(re, 64, 1), im)


def translate_kernel(box_id, lists, recv, factor, send, source, sums, send_v, idx, load_sems, store_sems):
    n_far, n_own = 48, 32
    me = box_id[0]

    def load(b):
        rows = pl.ds(pl.multiple_of(24 * b, 8), 24)
        away = lax.bitwise_xor(me, b)
        return pltpu.make_async_copy(lists.at[2 * (away & 3) + (away >> 2)], idx.at[rows], load_sems.at[b])

    for b in range(8):
        load(jnp.int32(b)).start()
    left = lax.broadcasted_iota(jnp.int32, (8, 128), 1) < 64
    even = lax.broadcasted_iota(jnp.int32, (8, 128), 0) % 2 == 0
    for b in range(8):

        def prepare(p, carry):
            v = recv[b, pl.ds(pl.multiple_of(8 * p, 8), 8), :]
            at = pl.multiple_of((b * n_own + p) * 24, 8)
            source[pl.ds(at, 8), :] = jnp.where(even, v, pltpu.roll(v, 1, 0))
            source[pl.ds(at + 8, 8), :] = jnp.where(even, pltpu.roll(v, 7, 0), v)
            return carry

        lax.fori_loop(0, n_own, prepare, 0, unroll=8)
        for q in range(4):
            v = recv[b, 256 + 8 * q : 264 + 8 * q, :]
            r = pltpu.roll(v, 64, 1)
            at = (b * n_own + 8 * q) * 24 + 16
            source[pl.ds(at, 8, stride=24), :] = jnp.where(left, v, r)
            source[pl.ds(at + 1, 8, stride=24), :] = jnp.where(left, r, v)

    def index(j, b, p):
        return pl.multiple_of(idx.at[pl.ds(j // 4, 169), pl.ds(n_own * (j % 4), n_own)][24 * b, p], 8)

    def some(i, b):
        acc = [[jnp.zeros((8, 128), jnp.float32) for _ in range(3)] for _ in range(8)]
        for j in range(n_far):
            for h in range(8):
                o = index(n_far + j, b, 8 * i + h)
                f = index(j, b, 8 * i + h)
                t = factor[pl.ds(o, 8), :]
                acc[h][0] += t * source[pl.ds(f, 8), :]
                acc[h][1] += t * source[pl.ds(f + 8, 8), :]
                acc[h][2] += factor[pl.ds(o + 8, 8), :] * source[pl.ds(f + 16, 8), :]
        for h in range(8):
            for k in range(3):
                sums[pl.ds(pl.multiple_of(24 * (b * n_own + 8 * i), 8) + 24 * h + 8 * k, 8), :] = acc[h][k]
        return b

    def finish(p, b):
        at = pl.multiple_of((b * n_own + p) * 24, 8)
        r = sums[pl.ds(at + 8, 8), :]
        r = jnp.where(even, -pltpu.roll(r, 7, 0), pltpu.roll(r, 1, 0))
        send_v[b, pl.ds(pl.multiple_of(8 * p, 8), 8), :] = sums[pl.ds(at, 8), :] + r
        return b

    def store(b):
        return pltpu.make_async_copy(send_v.at[pl.ds(b, 1)], send.at[pl.ds(b, 1)], store_sems.at[b])

    def box(b, carry):
        load(b).wait()
        lax.fori_loop(0, n_own // 8, some, b)
        lax.fori_loop(0, n_own, finish, b, unroll=8)
        for q in range(4):
            at = (b * n_own + 8 * q) * 24 + 16
            r = pltpu.roll(sums[pl.ds(at + 1, 8, stride=24), :], 64, 1)
            rows = slice(256 + 8 * q, 264 + 8 * q)
            send_v[b, rows, :] = sums[pl.ds(at, 8, stride=24), :] + jnp.where(left, -r, r)
        store(b).start()
        return carry

    lax.fori_loop(0, 8, box, 0)
    for b in range(8):
        store(b).wait()


def place_kernel(recv, out, last, out_v, sems):
    left = lax.broadcasted_iota(jnp.int32, (8, 128), 1) < 64
    copies = []
    for q in range(4):
        for r in range(4):
            rows = slice(256 + 8 * q, 264 + 8 * q)
            e, o = recv[2 * r, rows, :], recv[2 * r + 1, rows, :]
            at = 8 * 8 * q + 2 * r
            last[pl.ds(at, 8, stride=8), :] = jnp.where(left, e, pltpu.roll(o, 64, 1))
            last[pl.ds(at + 1, 8, stride=8), :] = jnp.where(left, pltpu.roll(e, 64, 1), o)

        def one(p, carry):
            base = pl.multiple_of(8 * p, 8)
            for at in range(36):
                rows = pl.ds(base + 2 * (at % 4), 2)
                v = recv[at // 4, rows, :] if at < 32 else last[rows, :]
                out_v[p, at // 3, :, 128 * (at % 3) : 128 * (at % 3) + 128] = v
            return carry

        lax.fori_loop(8 * q, 8 * q + 8, one, 0)
        some = pl.ds(8 * q, 8)
        copies.append(pltpu.make_async_copy(out_v.at[some], out.at[some], sems.at[q]))
        copies[-1].start()
    for copy in copies:
        copy.wait()


def phase_tables(samp, n_theta, n_phi):
    polar = np.concatenate([np.arange(12), np.arange(8, 12)])
    sign = np.where((np.arange(16) >= 8) & (np.arange(16) < 12), -1.0, 1.0).astype(np.float32)
    theta = (samp * 12 + polar).astype(jnp.float32) * (math.pi / n_theta) + 0.5 * math.pi / n_theta
    phi = np.arange(n_phi) * (2.0 * math.pi / n_phi)
    o = np.arange(8)
    sx, sy, sz = 1.0 - 2 * (o % 2), 1.0 - 2 * (o // 2 % 2), 1.0 - 2 * (o // 4)
    around = (sx[:, None] * np.cos(phi) + sy[:, None] * np.sin(phi)).astype(np.float32)
    angle = phase_scale * (
        jnp.sin(theta)[None, :, None] * around[:, None, :]
        + (sz.astype(np.float32)[:, None] * jnp.cos(theta)[None, :])[:, :, None]
    )
    return jnp.cos(angle), jnp.sin(angle) * sign[None, :, None]


def vmem():
    return pl.BlockSpec(memory_space=pltpu.VMEM)


def smem():
    return pl.BlockSpec(memory_space=pltpu.SMEM)


def held(x):
    return pltpu.with_memory_space_constraint(x, pltpu.VMEM)


def params(mib):
    return pltpu.CompilerParams(vmem_limit_bytes=mib * 2**20)


def anywhere():
    return pl.BlockSpec(memory_space=pl.ANY)


def far_away(x):
    return pltpu.with_memory_space_constraint(x, pltpu.HBM)


def shards(child_patterns, octants, parent_map, far_boxes, offsets, translation):
    n_box, n_samp = lax.axis_size("box"), lax.axis_size("samp")
    count, _, n_t1, n_p1 = child_patterns.shape
    n_off, _, band, n_p2 = translation.shape
    n_t2 = band * n_samp
    parents, n_far = far_boxes.shape
    box, samp = lax.axis_index("box"), lax.axis_index("samp")
    f32, bf16 = jnp.float32, jnp.bfloat16

    theta_table = lagrange_table(n_t1, n_t2, False).reshape(n_samp, band, n_t1)
    parts = [theta_table[:, 0:8].reshape(-1, n_t1), theta_table[:, 8:12].reshape(-1, n_t1)]
    theta_high, theta_low = high_low(np.concatenate(parts))
    phi_table = lagrange_table(n_p1, n_p2, True)
    first = np.arange(n_p2) * n_p1 // n_p2 - 2
    stencil = np.zeros((8, n_p2), np.float32)
    for i in range(6):
        stencil[i] = phi_table[np.arange(n_p2), (first + i) % n_p1]
    stencil[6] = first % n_p1

    sent = (n_samp, 48 * count + 8, 128)
    bands, token = pl.pallas_call(
        theta_kernel,
        in_specs=[anywhere()] * 4,
        out_specs=[anywhere(), vmem()],
        out_shape=[pltpu.HBM(sent, f32), jax.ShapeDtypeStruct((8, 128), f32)],
        scratch_shapes=[
            pltpu.VMEM((2, n_t2, n_t1), bf16),
            pltpu.VMEM(child_patterns.shape, f32),
            pltpu.VMEM(sent, f32),
            pltpu.SMEM((1, count), jnp.int32),
            pltpu.SemaphoreType.DMA((3 * count + 3,)),
        ],
        compiler_params=params(9),
        name="theta",
    )(far_away(octants.reshape(1, count)), far_away(theta_high), far_away(theta_low), far_away(child_patterns))
    bands = lax.all_to_all(bands, "samp", 0, 0)

    cos_part, sin_part = phase_tables(samp, n_t2, n_p2)
    lists = jnp.concatenate([far_boxes.T * 24, offsets.T * 16], 0).reshape(24, 128).astype(f32)
    factor, stencil, lists = pl.pallas_call(
        prepare_kernel,
        in_specs=[smem(), vmem(), vmem(), vmem(), anywhere()],
        out_specs=[vmem()] * 3,
        out_shape=[
            pltpu.VMEM((n_off, 16, 128), f32),
            jax.ShapeDtypeStruct(stencil.shape, f32),
            jax.ShapeDtypeStruct((24, 128), f32),
        ],
        scratch_shapes=[pltpu.VMEM((n_off, 5, 2, 128), f32), pltpu.SemaphoreType.DMA((5,))],
        compiler_params=params(6),
        cost_estimate=pl.CostEstimate(flops=10**7, bytes_accessed=10**7, transcendentals=0),
        name="prepare",
    )(box.reshape(1), token, lists, stencil, far_away(translation.transpose(0, 2, 1, 3)))
    pairs = [[(i, i ^ k) for i in range(n_box)] for k in range(n_box)]
    lists = jnp.stack([lists, lax.ppermute(lists, "box", pairs[4])])
    lists = jnp.concatenate([lists] + [lax.ppermute(lists, "box", pairs[k]) for k in (1, 2, 3)]).astype(jnp.int32)

    send = pl.pallas_call(
        phi_kernel,
        in_specs=[smem(), vmem()] + [anywhere()] * 3 + [vmem()],
        out_specs=vmem(),
        out_shape=pltpu.VMEM((n_box, 9 * parents, 128), f32),
        scratch_shapes=[
            pltpu.VMEM((parents, 24, n_p2), f32),
            pltpu.VMEM((2, 24 * count, n_p2), f32),
            pltpu.VMEM((parents * 72 + 64, 128), f32),
            pltpu.VMEM(cos_part.shape, f32),
            pltpu.VMEM(cos_part.shape, f32),
            pltpu.VMEM((n_samp + 8, 128), jnp.int32),
            pltpu.SMEM((n_samp + 8, 128), jnp.int32),
            pltpu.SemaphoreType.DMA((10,)),
        ],
        compiler_params=params(12),
        name="phi",
    )(
        parent_map[0], stencil, lists, far_away(cos_part), far_away(sin_part), held(bands),
    )

    everywhere = lax.all_to_all(send, "box", 0, 0)
    n_all = n_box * parents
    back = pl.pallas_call(
        translate_kernel,
        in_specs=[smem(), vmem(), vmem(), vmem()],
        out_specs=anywhere(),
        out_shape=pltpu.HBM((n_box, 9 * parents, 128), f32),
        scratch_shapes=[
            pltpu.VMEM((n_all * 24, 128), f32),
            pltpu.VMEM((n_all * 24, 128), f32),
            pltpu.VMEM((n_box, 9 * parents, 128), f32),
            pltpu.SMEM((24 * n_box, 128), jnp.int32),
            pltpu.SemaphoreType.DMA((n_box,)),
            pltpu.SemaphoreType.DMA((n_box,)),
        ],
        compiler_params=params(12),
        name="translate",
    )(box.reshape(1), lists, held(everywhere), held(factor.reshape(n_off * 16, 128)))
    back = lax.all_to_all(back, "box", 0, 0)
    shape = (parents, band, 2, n_p2)
    place = pl.pallas_call(
        place_kernel,
        in_specs=[vmem()],
        out_specs=anywhere(),
        out_shape=pltpu.HBM(shape, f32),
        scratch_shapes=[
            pltpu.VMEM((8 * parents + 8, 128), f32),
            pltpu.VMEM(shape, f32),
            pltpu.SemaphoreType.DMA((4,)),
        ],
        compiler_params=params(6),
        cost_estimate=pl.CostEstimate(flops=10**6, bytes_accessed=4 * 10**6, transcendentals=0),
        name="place",
    )
    outgoing, incoming = place(send), place(held(back))
    return outgoing.transpose(0, 2, 1, 3), incoming.transpose(0, 2, 1, 3)


def solution(mesh):
    in_specs = (
        P(("box", "samp"), None, None, None),
        P(("box", "samp")),
        P("box", None),
        P("box", None),
        P("box", None),
        P(None, None, "samp", None),
    )
    out_specs = (P("box", None, "samp", None), P("box", None, "samp", None))
    return jax.shard_map(shards, mesh=mesh, in_specs=in_specs, out_specs=out_specs, check_vma=False)
```

```python
import functools
import math

import jax
import jax.numpy as jnp
import numpy as np
from jax import lax
from jax.experimental import pallas as pl
from jax.experimental.pallas import tpu as pltpu
from jax.sharding import PartitionSpec as P

phase_scale = 12.0


def lagrange_table(n_old, n_new, periodic):
    rows = np.arange(n_new)
    if periodic:
        numer, denom = rows * n_old, n_new
    else:
        numer, denom = (2 * rows + 1) * n_old - n_new, 2 * n_new
    start = numer // denom - 2
    if not periodic:
        start = np.clip(start, 0, n_old - 6)
    position = numer / denom - start
    table = np.zeros((n_new, n_old))
    for node in range(6):
        weight = np.ones(n_new)
        for other in range(6):
            if other != node:
                weight = weight * (position - other) / (node - other)
        target = start + node
        if periodic:
            target = target % n_old
        table[rows, target] += weight
    return table


def high_low(table):
    table = table.astype(np.float32)
    high = table.astype(jnp.bfloat16)
    low = (table - high.astype(np.float32)).astype(jnp.bfloat16)
    return high, low


def split(x):
    high = x.astype(jnp.bfloat16)
    low = (x - high.astype(jnp.float32)).astype(jnp.bfloat16)
    return high, low


def dot3(a, b):
    f = functools.partial(jnp.dot, preferred_element_type=jnp.float32)
    return f(a[0], b[0]) + (f(a[0], b[1]) + f(a[1], b[0]))


def theta_kernel(octants, table_high, table_low, child, out, token, tables, kids, bands, kinds, sems):
    n_kids, n_samp = child.shape[0], out.shape[0]
    loads = [pltpu.make_async_copy(child.at[c], kids.at[c], sems.at[c]) for c in range(n_kids)]
    parts = [
        pltpu.make_async_copy(table, tables.at[i], sems.at[n_kids + i])
        for i, table in enumerate((table_high, table_low))
    ]
    for copy in parts:
        copy.start()
    small = pltpu.make_async_copy(octants, kinds, sems.at[n_kids + 2])
    small.start()
    for copy in loads:
        copy.start()
    small.wait()
    lane = lax.broadcasted_iota(jnp.int32, (8, 128), 1)
    v = jnp.zeros((8, 128), jnp.int32)
    for i in range(8):
        v = jnp.where(lane == i, kinds[0, i], v)
    v = v.astype(jnp.float32)
    for s in range(n_samp):
        bands[s, 384:392, :] = v
    token[...] = v
    stores = []

    def store(first, count):
        rows = pl.ds(first, count)
        stores.append(pltpu.make_async_copy(bands.at[:, rows], out.at[:, rows], sems.at[n_kids + 3 + len(stores)]))
        stores[-1].start()

    for copy in parts:
        copy.wait()
    table = jnp.concatenate([tables[0], tables[0], tables[1]], 1)
    for c in range(n_kids):
        loads[c].wait()
        high, low = split(jnp.concatenate([kids[c, 0], kids[c, 1]], 1))
        y = jnp.dot(table, jnp.concatenate([high, low, high], 0), preferred_element_type=jnp.float32)
        for s in range(n_samp):
            for half in range(2):
                at = 192 * half + 24 * c
                for k in range(2):
                    cols = slice(256 * k + 128 * half, 256 * k + 128 * half + 128)
                    bands[s, at + 8 * k : at + 8 * k + 8, :] = y[8 * s : 8 * s + 8, cols]
                    rest = y[128 + 4 * s : 132 + 4 * s, cols]
                    bands[s, at + 16 + 4 * k : at + 20 + 4 * k, :] = rest
        store(24 * c, 24)
        store(192 + 24 * c, 24 + 8 * (c == n_kids - 1))
    for copy in stores:
        copy.wait()


def prepare_kernel(box, token, lists, stencil, table, out, stencil_out, lists_out, raw, sems):
    me = box[0]
    n_off = table.shape[0]
    pair, half = me // 2, me % 2
    copies = []
    for q in range(5):
        at = 4 * me + q if q < 4 else 32 + pair
        lanes = pl.ds(pl.multiple_of(128 * (at % 3), 128), 128)
        copies.append(
            pltpu.make_async_copy(table.at[:, at // 3, :, lanes], raw.at[:, q], sems.at[q])
        )
        copies[-1].start()
    stencil_out[...] = stencil[...]
    lists_out[...] = lists[...]
    for copy in copies:
        copy.wait()
    left = lax.broadcasted_iota(jnp.int32, (1, 128), 1) < 64
    upper = jnp.full((1, 128), half, jnp.int32) == 1

    def one(i, carry):
        out[i, 0:8] = jnp.concatenate([raw[i, q] for q in range(4)], 0)
        re, im = raw[i, 4, 0:1], raw[i, 4, 1:2]
        x = jnp.where(left, re, pltpu.roll(im, 64, 1))
        y = jnp.where(left, pltpu.roll(re, 64, 1), im)
        out[i, 8:16] = jnp.broadcast_to(jnp.where(upper, y, x), (8, 128))
        return carry

    lax.fori_loop(0, n_off // 4, lambda i, c: [one(4 * i + u, c) for u in range(4)][-1], 0)


def phi_kernel(
    owners, stencil, lists, cos_hbm, sin_hbm, recv, send_v, total, fine, rows_v, cos_ref, sin_ref, kinds_v, kinds, sems
):
    loads = [pltpu.make_async_copy(a, b, sems.at[i]) for i, (a, b) in enumerate(((cos_hbm, cos_ref), (sin_hbm, sin_ref)))]
    for load in loads:
        load.start()
    for s in range(16):
        kinds_v[s : s + 1, :] = recv[s, 384:385, :].astype(jnp.int32)
    copy = pltpu.make_async_copy(kinds_v, kinds, sems.at[4])
    copy.start()
    total[...] = jnp.zeros_like(total)
    shape = (recv.shape[2] * 2, stencil.shape[1])
    node = (lax.broadcasted_iota(jnp.int32, shape, 0) - stencil[6:7, :].astype(jnp.int32)) & (shape[0] - 1)
    table = jnp.zeros(shape, jnp.float32)
    for i in range(6):
        table = jnp.where(node == i, stencil[i : i + 1, :], table)
    high, low = split(table)
    table = jnp.concatenate([high, high, low], 0)

    def product(s):
        high, low = split(jnp.concatenate([recv[s, 0:192, :], recv[s, 192:384, :]], 1))
        return jnp.dot(jnp.concatenate([high, low, high], 1), table, preferred_element_type=jnp.float32)

    def add(s, fine):
        for c in range(8):
            child = s * 8 + c
            owner, octant = owners[child], kinds[s, c]
            f = fine[24 * c : 24 * c + 24, :]
            cos_0, sin_0 = cos_ref[octant, 0:8], sin_ref[octant, 0:8]
            total[owner, 0:8] += cos_0 * f[0:8] - sin_0 * f[8:16]
            total[owner, 8:16] += sin_0 * f[0:8] + cos_0 * f[8:16]
            swapped = pltpu.roll(f[16:24], 4, 0)
            total[owner, 16:24] += cos_ref[octant, 8:16] * f[16:24] + sin_ref[octant, 8:16] * swapped

    fine[0] = product(0)
    for load in loads:
        load.wait()
    copy.wait()

    def two(i, carry):
        s = 2 * i
        fine[1] = product(s + 1)
        add(s, fine.at[0])
        fine[0] = product(lax.rem(s + 2, 16))
        add(s + 1, fine.at[1])
        return carry

    lax.fori_loop(0, 8, two, 0, unroll=4)

    def parent(p, carry):
        for l in range(3):
            v = total[p, :, 128 * l : 128 * l + 128]
            base = 72 * p + 2 * l
            rows_v[pl.ds(base, 8, stride=6), :] = v[0:8]
            rows_v[pl.ds(base + 1, 8, stride=6), :] = v[8:16]
            rows_v[pl.ds(base + 48, 4, stride=6), :] = v[16:20]
            rows_v[pl.ds(base + 49, 4, stride=6), :] = v[20:24]
        for d in range(8):
            at = pl.multiple_of(72 * p + 8 * d, 8)
            send_v[d, pl.ds(pl.multiple_of(8 * p, 8), 8), :] = rows_v[pl.ds(at, 8), :]
        return carry

    left = lax.broadcasted_iota(jnp.int32, (8, 128), 1) < 64
    for q in range(4):
        lax.fori_loop(8 * q, 8 * q + 8, parent, 0, unroll=4)
        for r in range(4):
            at = 72 * 8 * q + 64 + 2 * r
            re, im = rows_v[pl.ds(at, 8, stride=72), :], rows_v[pl.ds(at + 1, 8, stride=72), :]
            rows = slice(256 + 8 * q, 264 + 8 * q)
            send_v[2 * r, rows, :] = jnp.where(left, re, pltpu.roll(im, 64, 1))
            send_v[2 * r + 1, rows, :] = jnp.where(left, pltpu.roll(re, 64, 1), im)


def translate_kernel(box_id, lists, recv, factor, send, source, sums, send_v, idx, load_sems, store_sems):
    n_far, n_own = 48, 32
    me = box_id[0]

    def load(b):
        rows = pl.ds(pl.multiple_of(24 * b, 8), 24)
        away = lax.bitwise_xor(me, b)
        return pltpu.make_async_copy(lists.at[2 * (away & 3) + (away >> 2)], idx.at[rows], load_sems.at[b])

    for b in range(8):
        load(jnp.int32(b)).start()
    left = lax.broadcasted_iota(jnp.int32, (8, 128), 1) < 64
    even = lax.broadcasted_iota(jnp.int32, (8, 128), 0) % 2 == 0
    for b in range(8):

        def prepare(p, carry):
            v = recv[b, pl.ds(pl.multiple_of(8 * p, 8), 8), :]
            at = pl.multiple_of((b * n_own + p) * 24, 8)
            source[pl.ds(at, 8), :] = jnp.where(even, v, pltpu.roll(v, 1, 0))
            source[pl.ds(at + 8, 8), :] = jnp.where(even, pltpu.roll(v, 7, 0), v)
            return carry

        lax.fori_loop(0, n_own, prepare, 0, unroll=8)
        for q in range(4):
            v = recv[b, 256 + 8 * q : 264 + 8 * q, :]
            r = pltpu.roll(v, 64, 1)
            at = (b * n_own + 8 * q) * 24 + 16
            source[pl.ds(at, 8, stride=24), :] = jnp.where(left, v, r)
            source[pl.ds(at + 1, 8, stride=24), :] = jnp.where(left, r, v)

    def index(j, b, p):
        return pl.multiple_of(idx.at[pl.ds(j // 4, 169), pl.ds(n_own * (j % 4), n_own)][24 * b, p], 8)

    def some(i, b):
        acc = [[jnp.zeros((8, 128), jnp.float32) for _ in range(3)] for _ in range(8)]
        for j in range(n_far):
            for h in range(8):
                o = index(n_far + j, b, 8 * i + h)
                f = index(j, b, 8 * i + h)
                t = factor[pl.ds(o, 8), :]
                acc[h][0] += t * source[pl.ds(f, 8), :]
                acc[h][1] += t * source[pl.ds(f + 8, 8), :]
                acc[h][2] += factor[pl.ds(o + 8, 8), :] * source[pl.ds(f + 16, 8), :]
        for h in range(8):
            for k in range(3):
                sums[pl.ds(pl.multiple_of(24 * (b * n_own + 8 * i), 8) + 24 * h + 8 * k, 8), :] = acc[h][k]
        return b

    def finish(p, b):
        at = pl.multiple_of((b * n_own + p) * 24, 8)
        r = sums[pl.ds(at + 8, 8), :]
        r = jnp.where(even, -pltpu.roll(r, 7, 0), pltpu.roll(r, 1, 0))
        send_v[b, pl.ds(pl.multiple_of(8 * p, 8), 8), :] = sums[pl.ds(at, 8), :] + r
        return b

    def store(b):
        return pltpu.make_async_copy(send_v.at[pl.ds(b, 1)], send.at[pl.ds(b, 1)], store_sems.at[b])

    def box(b, carry):
        load(b).wait()
        lax.fori_loop(0, n_own // 8, some, b)
        lax.fori_loop(0, n_own, finish, b, unroll=8)
        for q in range(4):
            at = (b * n_own + 8 * q) * 24 + 16
            r = pltpu.roll(sums[pl.ds(at + 1, 8, stride=24), :], 64, 1)
            rows = slice(256 + 8 * q, 264 + 8 * q)
            send_v[b, rows, :] = sums[pl.ds(at, 8, stride=24), :] + jnp.where(left, -r, r)
        store(b).start()
        return carry

    lax.fori_loop(0, 8, box, 0)
    for b in range(8):
        store(b).wait()


def place_kernel(recv, out, last, out_v, sems):
    left = lax.broadcasted_iota(jnp.int32, (8, 128), 1) < 64
    copies = []
    for q in range(4):
        for r in range(4):
            rows = slice(256 + 8 * q, 264 + 8 * q)
            e, o = recv[2 * r, rows, :], recv[2 * r + 1, rows, :]
            at = 8 * 8 * q + 2 * r
            last[pl.ds(at, 8, stride=8), :] = jnp.where(left, e, pltpu.roll(o, 64, 1))
            last[pl.ds(at + 1, 8, stride=8), :] = jnp.where(left, pltpu.roll(e, 64, 1), o)

        def one(p, carry):
            base = pl.multiple_of(8 * p, 8)
            for at in range(36):
                rows = pl.ds(base + 2 * (at % 4), 2)
                v = recv[at // 4, rows, :] if at < 32 else last[rows, :]
                out_v[p, at // 3, :, 128 * (at % 3) : 128 * (at % 3) + 128] = v
            return carry

        lax.fori_loop(8 * q, 8 * q + 8, one, 0, unroll=4)
        some = pl.ds(8 * q, 8)
        copies.append(pltpu.make_async_copy(out_v.at[some], out.at[some], sems.at[q]))
        copies[-1].start()
    for copy in copies:
        copy.wait()


def phase_tables(samp, n_theta, n_phi):
    polar = np.concatenate([np.arange(12), np.arange(8, 12)])
    sign = np.where((np.arange(16) >= 8) & (np.arange(16) < 12), -1.0, 1.0).astype(np.float32)
    theta = (samp * 12 + polar).astype(jnp.float32) * (math.pi / n_theta) + 0.5 * math.pi / n_theta
    phi = np.arange(n_phi) * (2.0 * math.pi / n_phi)
    o = np.arange(8)
    sx, sy, sz = 1.0 - 2 * (o % 2), 1.0 - 2 * (o // 2 % 2), 1.0 - 2 * (o // 4)
    around = (sx[:, None] * np.cos(phi) + sy[:, None] * np.sin(phi)).astype(np.float32)
    angle = phase_scale * (
        jnp.sin(theta)[None, :, None] * around[:, None, :]
        + (sz.astype(np.float32)[:, None] * jnp.cos(theta)[None, :])[:, :, None]
    )
    return jnp.cos(angle), jnp.sin(angle) * sign[None, :, None]


def vmem():
    return pl.BlockSpec(memory_space=pltpu.VMEM)


def smem():
    return pl.BlockSpec(memory_space=pltpu.SMEM)


def held(x):
    return pltpu.with_memory_space_constraint(x, pltpu.VMEM)


def params(mib):
    return pltpu.CompilerParams(vmem_limit_bytes=mib * 2**20)


def anywhere():
    return pl.BlockSpec(memory_space=pl.ANY)


def far_away(x):
    return pltpu.with_memory_space_constraint(x, pltpu.HBM)


def shards(child_patterns, octants, parent_map, far_boxes, offsets, translation):
    n_box, n_samp = lax.axis_size("box"), lax.axis_size("samp")
    count, _, n_t1, n_p1 = child_patterns.shape
    n_off, _, band, n_p2 = translation.shape
    n_t2 = band * n_samp
    parents, n_far = far_boxes.shape
    box, samp = lax.axis_index("box"), lax.axis_index("samp")
    f32, bf16 = jnp.float32, jnp.bfloat16

    theta_table = lagrange_table(n_t1, n_t2, False).reshape(n_samp, band, n_t1)
    parts = [theta_table[:, 0:8].reshape(-1, n_t1), theta_table[:, 8:12].reshape(-1, n_t1)]
    theta_high, theta_low = high_low(np.concatenate(parts))
    phi_table = lagrange_table(n_p1, n_p2, True)
    first = np.arange(n_p2) * n_p1 // n_p2 - 2
    stencil = np.zeros((8, n_p2), np.float32)
    for i in range(6):
        stencil[i] = phi_table[np.arange(n_p2), (first + i) % n_p1]
    stencil[6] = first % n_p1

    sent = (n_samp, 48 * count + 8, 128)
    bands, token = pl.pallas_call(
        theta_kernel,
        in_specs=[anywhere()] * 4,
        out_specs=[anywhere(), vmem()],
        out_shape=[pltpu.HBM(sent, f32), jax.ShapeDtypeStruct((8, 128), f32)],
        scratch_shapes=[
            pltpu.VMEM((2, n_t2, n_t1), bf16),
            pltpu.VMEM(child_patterns.shape, f32),
            pltpu.VMEM(sent, f32),
            pltpu.SMEM((1, count), jnp.int32),
            pltpu.SemaphoreType.DMA((3 * count + 3,)),
        ],
        compiler_params=params(9),
        name="theta",
    )(far_away(octants.reshape(1, count)), far_away(theta_high), far_away(theta_low), far_away(child_patterns))
    bands = lax.all_to_all(bands, "samp", 0, 0)

    cos_part, sin_part = phase_tables(samp, n_t2, n_p2)
    lists = jnp.concatenate([far_boxes.T * 24, offsets.T * 16], 0).reshape(24, 128).astype(f32)
    factor, stencil, lists = pl.pallas_call(
        prepare_kernel,
        in_specs=[smem(), vmem(), vmem(), vmem(), anywhere()],
        out_specs=[vmem()] * 3,
        out_shape=[
            pltpu.VMEM((n_off, 16, 128), f32),
            jax.ShapeDtypeStruct(stencil.shape, f32),
            jax.ShapeDtypeStruct((24, 128), f32),
        ],
        scratch_shapes=[pltpu.VMEM((n_off, 5, 2, 128), f32), pltpu.SemaphoreType.DMA((5,))],
        compiler_params=params(6),
        cost_estimate=pl.CostEstimate(flops=10**7, bytes_accessed=10**7, transcendentals=0),
        name="prepare",
    )(box.reshape(1), token, lists, stencil, far_away(translation.transpose(0, 2, 1, 3)))
    pairs = [[(i, i ^ k) for i in range(n_box)] for k in range(n_box)]
    lists = jnp.stack([lists, lax.ppermute(lists, "box", pairs[4])])
    lists = jnp.concatenate([lists] + [lax.ppermute(lists, "box", pairs[k]) for k in (1, 2, 3)]).astype(jnp.int32)

    send = pl.pallas_call(
        phi_kernel,
        in_specs=[smem(), vmem()] + [anywhere()] * 3 + [vmem()],
        out_specs=vmem(),
        out_shape=pltpu.VMEM((n_box, 9 * parents, 128), f32),
        scratch_shapes=[
            pltpu.VMEM((parents, 24, n_p2), f32),
            pltpu.VMEM((2, 24 * count, n_p2), f32),
            pltpu.VMEM((parents * 72 + 64, 128), f32),
            pltpu.VMEM(cos_part.shape, f32),
            pltpu.VMEM(cos_part.shape, f32),
            pltpu.VMEM((n_samp + 8, 128), jnp.int32),
            pltpu.SMEM((n_samp + 8, 128), jnp.int32),
            pltpu.SemaphoreType.DMA((10,)),
        ],
        compiler_params=params(12),
        name="phi",
    )(
        parent_map[0], stencil, lists, far_away(cos_part), far_away(sin_part), held(bands),
    )

    everywhere = lax.all_to_all(send, "box", 0, 0)
    n_all = n_box * parents
    back = pl.pallas_call(
        translate_kernel,
        in_specs=[smem(), vmem(), vmem(), vmem()],
        out_specs=anywhere(),
        out_shape=pltpu.HBM((n_box, 9 * parents, 128), f32),
        scratch_shapes=[
            pltpu.VMEM((n_all * 24, 128), f32),
            pltpu.VMEM((n_all * 24, 128), f32),
            pltpu.VMEM((n_box, 9 * parents, 128), f32),
            pltpu.SMEM((24 * n_box, 128), jnp.int32),
            pltpu.SemaphoreType.DMA((n_box,)),
            pltpu.SemaphoreType.DMA((n_box,)),
        ],
        compiler_params=params(12),
        name="translate",
    )(box.reshape(1), lists, held(everywhere), held(factor.reshape(n_off * 16, 128)))
    back = lax.all_to_all(back, "box", 0, 0)
    shape = (parents, band, 2, n_p2)
    place = pl.pallas_call(
        place_kernel,
        in_specs=[vmem()],
        out_specs=anywhere(),
        out_shape=pltpu.HBM(shape, f32),
        scratch_shapes=[
            pltpu.VMEM((8 * parents + 8, 128), f32),
            pltpu.VMEM(shape, f32),
            pltpu.SemaphoreType.DMA((4,)),
        ],
        compiler_params=params(6),
        cost_estimate=pl.CostEstimate(flops=10**6, bytes_accessed=4 * 10**6, transcendentals=0),
        name="place",
    )
    outgoing, incoming = place(send), place(held(back))
    return outgoing.transpose(0, 2, 1, 3), incoming.transpose(0, 2, 1, 3)


def solution(mesh):
    in_specs = (
        P(("box", "samp"), None, None, None),
        P(("box", "samp")),
        P("box", None),
        P("box", None),
        P("box", None),
        P(None, None, "samp", None),
    )
    out_specs = (P("box", None, "samp", None), P("box", None, "samp", None))
    return jax.shard_map(shards, mesh=mesh, in_specs=in_specs, out_specs=out_specs, check_vma=False)
```
